32 devices in a mesh: groups: 2 (over y), seq: 4 (over z), sub: 2 (over x), rep: 2 (over core).
Axes of the slice: x: 2, y: 2, z: 4, core: 2. Of those that a mesh axis runs over, the one named last changes fastest.
Arguments:
- moe_input: bfloat16 [2048, 2048], P(('groups', 'seq'), ('sub', 'rep')), parts along dimension 0, may hold values from -6 to 6
- upstream: bfloat16 [2048, 2048], P(('groups', 'seq'), ('sub', 'rep')), parts along dimension 0, may hold values from -6 to 6
- expert_ids: int32 [2048, 2], P(('groups', 'seq')), parts along dimension 0, may hold values from 0 to 7, all different within a row; in each aligned block of 256 rows (0 to 255, 256 to 511, ...) at most 96 rows name the same one
- router_weight: float32 [2048, 2], P(('groups', 'seq')), parts along dimension 0, may hold values from 0.05 to 1
- w_gate: bfloat16 [8, 2048, 768], P('seq', ('sub', 'rep')), may hold values from -0.125 to 0.125
- w_up: bfloat16 [8, 2048, 768], P('seq', ('sub', 'rep')), may hold values from -0.125 to 0.125
- w_down: bfloat16 [8, 768, 2048], P('seq', None, ('sub', 'rep')), may hold values from -0.21875 to 0.21875
- out_proj: bfloat16 [2048, 2048], P(('sub', 'rep')), may hold values from -0.125 to 0.125
- query: bfloat16 [2048, 2048], P(('groups', 'seq'), ('sub', 'rep')), parts along dimension 0, may hold values from -8 to 8
- key_in: bfloat16 [2048, 2048], P(('groups', 'seq'), ('sub', 'rep')), parts along dimension 0, may hold values from -8 to 8
- value: bfloat16 [2048, 2048], P(('groups', 'seq'), ('sub', 'rep')), parts along dimension 0, may hold values from -6 to 6
Outputs:
- resid_grad: bfloat16 [2048, 2048], P(('groups', 'seq'), ('sub', 'rep')), parts along dimension 0
- query_grad: bfloat16 [2048, 2048], P(('groups', 'seq'), ('sub', 'rep')), parts along dimension 0
- key_grad: bfloat16 [2048, 2048], P(('groups', 'seq'), ('sub', 'rep')), parts along dimension 0
- value_grad: bfloat16 [2048, 2048], P(('groups', 'seq'), ('sub', 'rep')), parts along dimension 0
The draws below stay inside these ranges and needn't reach their ends.
There are 2 independent parts, one for each index of `groups`. The reference program is written for one: setup_inputs(seed, part) draws one part's arguments, and reference() takes and returns one part's arrays. A program takes and returns all parts, laid end to end along the dimension named above; an argument that names none is the same for every part. Nothing has to cross between parts.
Inputs may be any that keep to these rules, and one draw needn't show every extreme that they name: `expert_ids`: each row names two different experts. In each aligned block of 256 rows (the rows of one index of seq) no expert is named by more than 96 rows, a bound that some block reaches.
All inputs are finite; a program needn't handle non-finite values.
Results may differ from the reference program's by a relative error of at most 0.02.
Values may be sent and summed in bfloat16 or wider, within the bound.
A program may use at most 64 MiB of HBM per device.

```python
import math
import jax
import jax.numpy as jnp
import numpy as np
from jax import lax

D = 2048
FF = 768
HEADS = 16
HEAD_DIM = 128
WINDOW = 128
TOK_SEQ = 256
EXPERTS = 8
TOKENS = 1024
CAP = 96
N_SEQ = 4
N_SUB = 2
N_REP = 2


def paired_rows(key):
    first, second = jax.random.split(jax.random.fold_in(key, 11), 2)
    queries = jax.random.truncated_normal(first, -6.0, 6.0, (TOKENS, D), jnp.float32)
    keys = jax.random.truncated_normal(second, -6.0, 6.0, (TOKENS, D), jnp.float32)
    return (queries, keys)


def draw_query(key, part):
    return paired_rows(key)[0].astype(jnp.bfloat16)


def draw_key_in(key, part):
    return paired_rows(key)[1].astype(jnp.bfloat16)


def shard_levels(own_key, dims, cuts, least, high):
    level = 1.0
    for position, parts in cuts:
        draws = jax.random.uniform(jax.random.fold_in(jax.random.fold_in(own_key, 6), position), (parts,), jnp.float32, least / len(cuts), high / len(cuts))
        level = level * jnp.repeat(jnp.exp(draws), dims[position] // parts).reshape((-1,) + (1,) * (len(dims) - 1 - position))
    return level


def assign_block(own_key, own, number, rows, count, top, bound, lean):
    ranking = jax.random.permutation(own_key, count)
    crowded, usual = portions_of(count, rows * top, bound, lean, True), portions_of(count, rows * top, bound, lean, False)
    places = jnp.arange(count)

    def named(sizes, offset_by):
        used = int((sizes > 0).sum())
        fixed = max(1, used // 4)
        shifted = fixed + (places - fixed + offset_by * (used - fixed)) % max(1, count - fixed)
        return jnp.zeros((count,), jnp.int32).at[ranking[jnp.where(places < fixed, places, shifted)]].set(jnp.asarray(sizes, jnp.int32))

    sizes = jnp.where(number % 4 == 0, named(crowded, number // 4), named(usual, number - number // 4 - 1))
    mixed = jax.random.permutation(jax.random.fold_in(own, 3), count)
    donor, sink = mixed[0:count // 2 * 2:2], mixed[1:count // 2 * 2:2]
    room = jnp.minimum(sizes[donor] - 1, bound - sizes[sink]) // 2
    room = jnp.where((donor == ranking[0]) | (sink == ranking[0]) | (sizes[sink] == 0), 0, jnp.maximum(room, 0))
    shifted = jax.random.randint(jax.random.fold_in(own, 4), (count // 2,), 0, 1 << 20) % (room + 1)
    sizes = sizes.at[donor].add(-shifted).at[sink].add(shifted)
    members = jnp.searchsorted(jnp.cumsum(sizes), jnp.arange(rows * top), side="right").astype(jnp.int32)
    grid = members.reshape(top, rows).T
    grid = grid[jax.random.permutation(jax.random.fold_in(own, 1), rows)]
    offset_by = jax.random.randint(jax.random.fold_in(own, 2), (rows, 1), 0, top)
    return jnp.take_along_axis(grid, (jnp.arange(top)[None, :] + offset_by) % top, axis=1)


def portions_of(number_of, total, bound, skew, full):
    weights = [(1 << 20) // math.isqrt(grade ** skew) + 1 for grade in range(1, number_of + 1)]
    largest = bound if full else min(bound, max(-(-total // number_of), total * weights[0] // sum(weights)))
    least = 1 if total - largest >= number_of - 1 else 0
    counts, surplus = [largest] + [least] * (number_of - 1), total - largest - least * (number_of - 1)
    while surplus > 0:
        free = [i for i in range(1, number_of) if counts[i] < largest] or [i for i in range(1, number_of) if counts[i] < bound]
        mass, remaining = sum([weights[i] for i in free]), surplus
        for i in free:
            more = min(bound - counts[i], max(1, remaining * weights[i] // mass), surplus)
            counts[i] = counts[i] + more
            surplus = surplus - more
    return np.array(counts)


def noise(rng, dims, width, bound, cuts=(), kind=jnp.bfloat16):
    entries = jax.random.normal(rng, dims, jnp.float32) * width
    if len(cuts) > 0:
        entries = shard_levels(rng, dims, cuts, -0.22, 0.18) * entries
    return jnp.clip(entries, min=-bound, max=bound).astype(kind)


def setup_inputs(seed: int = 0, part: int = 0) -> dict:
    seeds = jax.random.split(jax.random.key(seed), 12)
    part_keys = jax.random.split(jax.random.fold_in(seeds[11], part), 12)
    moe_input = noise(part_keys[0], (TOKENS, D), 1.0, 6.0, ((0, 4), (1, 4)))
    upstream = noise(part_keys[1], (TOKENS, D), 1.0, 6.0, ((0, 4), (1, 4)))
    expert_ids_keys = jax.random.split(jax.random.fold_in(part_keys[2], 1), TOKENS // TOK_SEQ)
    expert_ids_turns = jax.random.permutation(jax.random.fold_in(part_keys[2], 3), TOKENS // TOK_SEQ)
    expert_ids = jax.vmap(lambda own, number: assign_block(jax.random.fold_in(part_keys[2], 2), own, number, TOK_SEQ, EXPERTS, 2, CAP, 2))(expert_ids_keys, expert_ids_turns).reshape((TOKENS, 2))
    router_weight = jnp.clip(jnp.exp(math.log(1.0) - 2.9957323 * jax.random.uniform(part_keys[3], (TOKENS, 2), jnp.float32) ** shard_levels(part_keys[3], (TOKENS, 2), ((0, 4),), -0.2, 0.2)), 0.05, 1.0)
    w_gate = noise(seeds[4], (EXPERTS, D, FF), D ** -0.5, 0.125, ((0, 4), (1, 4)))
    w_up = noise(seeds[5], (EXPERTS, D, FF), D ** -0.5, 0.125, ((0, 4), (1, 4)))
    w_down = noise(seeds[6], (EXPERTS, FF, D), FF ** -0.5, 0.21875, ((0, 4), (2, 4)))
    out_proj = noise(seeds[7], (D, D), D ** -0.5, 0.125, ((0, 4),))
    query = draw_query(jax.random.fold_in(jax.random.fold_in(seeds[11], part), 71), part)
    key_in = draw_key_in(jax.random.fold_in(jax.random.fold_in(seeds[11], part), 71), part)
    value = noise(part_keys[10], (TOKENS, D), 1.0, 6.0, ((0, 4), (1, 4)))
    return dict(moe_input=moe_input, upstream=upstream, expert_ids=expert_ids, router_weight=router_weight, w_gate=w_gate, w_up=w_up, w_down=w_down, out_proj=out_proj, query=query, key_in=key_in, value=value)


exact_precision = lax.Precision.HIGHEST

def lower_precision_cast(values_in):
    return lax.optimization_barrier(values_in.astype(jnp.bfloat16)).astype(jnp.float32)

def silu_grads(pre_gate, pre_up, hidden_grad):
    sigmoid_gate = jax.nn.sigmoid(pre_gate)
    gate_grad = hidden_grad * pre_up * sigmoid_gate * (1.0 + pre_gate * (1.0 - sigmoid_gate))
    up_grad = hidden_grad * pre_gate * sigmoid_gate
    return (lower_precision_cast(gate_grad), lower_precision_cast(up_grad))

def expert_grad(operands):
    slot_input, slot_grad, gate_matrix, up_matrix, down_matrix = operands
    pieces = N_SUB * N_REP
    slot_count = slot_input.shape[0]
    width_part = D // pieces
    inputs_split = slot_input.astype(jnp.float32).reshape(slot_count, pieces, width_part)
    grads_split = slot_grad.astype(jnp.float32).reshape(slot_count, pieces, width_part)
    gate_split = gate_matrix.astype(jnp.float32).reshape(pieces, width_part, FF)
    up_split = up_matrix.astype(jnp.float32).reshape(pieces, width_part, FF)
    down_split = down_matrix.astype(jnp.float32).reshape(FF, pieces, width_part)
    pre_gate = lax.optimization_barrier(jnp.sum(lower_precision_cast(jnp.einsum('nfd,fdh->fnh', inputs_split, gate_split, precision=exact_precision)), axis=0))
    pre_up = lax.optimization_barrier(jnp.sum(lower_precision_cast(jnp.einsum('nfd,fdh->fnh', inputs_split, up_split, precision=exact_precision)), axis=0))
    hidden_grad = lax.optimization_barrier(jnp.sum(lower_precision_cast(jnp.einsum('nfd,hfd->fnh', grads_split, down_split, precision=exact_precision)), axis=0))
    gate_grad, up_grad = silu_grads(pre_gate, pre_up, hidden_grad)
    input_grad = jnp.einsum('nh,dh->nd', gate_grad, gate_matrix.astype(jnp.float32), precision=exact_precision)
    input_grad = input_grad + jnp.einsum('nh,dh->nd', up_grad, up_matrix.astype(jnp.float32), precision=exact_precision)
    return input_grad.astype(jnp.bfloat16)

def moe_backward(moe_input, upstream, expert_ids, router_weight, w_gate, w_up, w_down):
    block_pairs = expert_ids.reshape(N_SEQ, 2 * TOK_SEQ)
    one_hot = (block_pairs[:, :, None] == jnp.arange(EXPERTS, dtype=jnp.int32)[None, None, :]).astype(jnp.int32)
    slot_rank = lax.optimization_barrier(jnp.sum((jnp.cumsum(one_hot, axis=1) - one_hot) * one_hot, axis=2))
    block_start = jnp.arange(N_SEQ, dtype=jnp.int32)[:, None] * (EXPERTS * CAP)
    flat_slot = (block_start + block_pairs * CAP + slot_rank).reshape(-1).astype(jnp.int32)
    slot_owner = jnp.zeros((N_SEQ * EXPERTS * CAP,), jnp.int32).at[flat_slot].set(jnp.arange(2 * TOKENS, dtype=jnp.int32) + 1)
    slot_owner = slot_owner.reshape(N_SEQ, EXPERTS, CAP).transpose(1, 0, 2).reshape(EXPERTS, N_SEQ * CAP)
    live_slot = (slot_owner > 0)[:, :, None]
    token_row = jnp.maximum(slot_owner - 1, 0) // 2
    slot_input = jnp.where(live_slot, moe_input[token_row], jnp.zeros((), jnp.bfloat16))
    slot_grad = jnp.where(live_slot, upstream[token_row], jnp.zeros((), jnp.bfloat16))
    slot_out = lax.map(expert_grad, (slot_input, slot_grad, w_gate, w_up, w_down))
    slot_out = slot_out.reshape(EXPERTS, N_SEQ, CAP, D).transpose(1, 0, 2, 3).reshape(N_SEQ * EXPERTS * CAP, D)
    pair_grads = slot_out[flat_slot].astype(jnp.float32) * router_weight.reshape(-1)[:, None]
    combined = upstream.astype(jnp.float32) + lax.optimization_barrier(jnp.sum(pair_grads.reshape(TOKENS, 2, D), axis=1))
    return combined.astype(jnp.bfloat16)

def window_single(queries, keys_ext, values_ext, out_grad, first_key):
    row_count = queries.shape[0]
    key_count = keys_ext.shape[0]
    scaling = HEAD_DIM ** (-0.5)
    query_pos = lax.broadcasted_iota(jnp.int32, (row_count, key_count), 0)
    key_pos = lax.broadcasted_iota(jnp.int32, (row_count, key_count), 1)
    allowed = (key_pos > query_pos) & (key_pos <= query_pos + WINDOW) & (key_pos + first_key >= 0)
    scores = jnp.where(allowed, jnp.dot(queries, keys_ext.T, precision=exact_precision) * scaling, -jnp.inf)
    highest = lax.optimization_barrier(jnp.max(scores, axis=1, keepdims=True))
    weights = jnp.exp(scores - highest)
    softmax_probs = weights / lax.optimization_barrier(jnp.sum(weights, axis=1, keepdims=True))
    probs_low = lower_precision_cast(softmax_probs)
    attended = jnp.dot(probs_low, values_ext, precision=exact_precision)
    centre = lax.optimization_barrier(jnp.sum(out_grad * attended, axis=1))
    prob_grad = jnp.dot(out_grad, values_ext.T, precision=exact_precision)
    score_grad = lower_precision_cast(softmax_probs * (prob_grad - centre[:, None]))
    win_query = jnp.dot(score_grad, keys_ext, precision=exact_precision) * scaling
    win_key = jnp.dot(score_grad.T, queries, precision=exact_precision) * scaling
    win_value = jnp.dot(probs_low.T, out_grad, precision=exact_precision)
    return (win_query, win_key, win_value)

def head_backward(operands):
    queries, keys, values, out_grad = operands
    block_shape = (N_SEQ, TOK_SEQ, HEAD_DIM)
    query_blocks = queries.astype(jnp.float32).reshape(block_shape)
    key_tiles = keys.astype(jnp.float32).reshape(block_shape)
    value_tiles = values.astype(jnp.float32).reshape(block_shape)
    gradient_tiles = out_grad.astype(jnp.float32).reshape(block_shape)
    state_local = jnp.einsum('nsd,nse->nde', key_tiles, value_tiles, precision=exact_precision)
    grad_local = jnp.einsum('nsd,nse->nde', query_blocks, gradient_tiles, precision=exact_precision)
    preceding_state = jnp.cumsum(state_local, axis=0) - state_local
    gradient_following = jnp.cumsum(grad_local[::-1], axis=0)[::-1] - grad_local
    causal_masking = (lax.broadcasted_iota(jnp.int32, (TOK_SEQ, TOK_SEQ), 0) >= lax.broadcasted_iota(jnp.int32, (TOK_SEQ, TOK_SEQ), 1))[None]
    value_products = lower_precision_cast(jnp.where(causal_masking, jnp.einsum('zct,zgt->zcg', gradient_tiles, value_tiles, precision=exact_precision), 0.0))
    query_products = lower_precision_cast(jnp.where(causal_masking, jnp.einsum('nid,njd->nij', query_blocks, key_tiles, precision=exact_precision), 0.0))
    linear_branch_scale = (HEAD_DIM * TOKENS) ** (-0.5)
    linear_query = linear_branch_scale * (jnp.einsum('qxz,qtz->qxt', gradient_tiles, preceding_state, precision=exact_precision) + jnp.einsum('mce,met->mct', value_products, key_tiles, precision=exact_precision))
    lin_key = linear_branch_scale * (jnp.einsum('nje,nde->njd', value_tiles, gradient_following, precision=exact_precision) + jnp.einsum('nij,nid->njd', value_products, query_blocks, precision=exact_precision))
    linear_value = linear_branch_scale * (jnp.einsum('xoq,xqz->xoz', key_tiles, gradient_following, precision=exact_precision) + jnp.einsum('wvg,wvk->wgk', query_products, gradient_tiles, precision=exact_precision))
    halo_zeros = jnp.zeros((1, WINDOW, HEAD_DIM), jnp.float32)
    keys_ext = jnp.concatenate([jnp.concatenate([halo_zeros, key_tiles[:-1, TOK_SEQ - WINDOW:]], axis=0), key_tiles], axis=1)
    values_ext = jnp.concatenate([jnp.concatenate([halo_zeros, value_tiles[:-1, TOK_SEQ - WINDOW:]], axis=0), value_tiles], axis=1)
    first_key = jnp.arange(N_SEQ, dtype=jnp.int32) * TOK_SEQ - WINDOW
    win_query, key_ext_grad, value_ext_grad = jax.vmap(window_single)(query_blocks, keys_ext, values_ext, gradient_tiles, first_key)
    padding = jnp.zeros((N_SEQ, TOK_SEQ - WINDOW, HEAD_DIM), jnp.float32)
    carried_key = jnp.concatenate([key_ext_grad[1:, :WINDOW], halo_zeros], axis=0)
    carried_value = jnp.concatenate([value_ext_grad[1:, :WINDOW], halo_zeros], axis=0)
    win_key = key_ext_grad[:, WINDOW:] + jnp.concatenate([padding, carried_key], axis=1)
    win_value = value_ext_grad[:, WINDOW:] + jnp.concatenate([padding, carried_value], axis=1)
    query_grad = (linear_query + win_query).astype(jnp.bfloat16).reshape(TOKENS, HEAD_DIM)
    key_grad = (lin_key + win_key).astype(jnp.bfloat16).reshape(TOKENS, HEAD_DIM)
    value_grad = (linear_value + win_value).astype(jnp.bfloat16).reshape(TOKENS, HEAD_DIM)
    return (query_grad, key_grad, value_grad)

def by_heads(matrix):
    return matrix.reshape(TOKENS, HEADS, HEAD_DIM).transpose(1, 0, 2)

def from_heads(stacked):
    return stacked.transpose(1, 0, 2).reshape(TOKENS, D)

def reference(moe_input, upstream, expert_ids, router_weight, w_gate, w_up, w_down, out_proj, query, key_in, value):
    resid_grad = moe_backward(moe_input, upstream, expert_ids, router_weight, w_gate, w_up, w_down)
    head_grad = jnp.dot(resid_grad, out_proj.T, preferred_element_type=jnp.float32).astype(jnp.bfloat16)
    query_grad, key_grad, value_grad = lax.map(head_backward, (by_heads(query), by_heads(key_in), by_heads(value), by_heads(head_grad)))
    return (resid_grad, from_heads(query_grad), from_heads(key_grad), from_heads(value_grad))
```

```python
import functools

import jax
import jax.numpy as jnp
from jax import lax
from jax.experimental import pallas as pl
from jax.experimental.pallas import tpu as pltpu
from jax.sharding import PartitionSpec as P

HEAD_DIM = 128
WINDOW = 128
MESH = pl.DeviceIdType.MESH
F32 = jnp.float32
BF16 = jnp.bfloat16


def entering(shard, axis, combine, identity, reverse):
    length, index = (lax.axis_size(axis), lax.axis_index(axis))
    everything = lax.all_gather(shard.astype(jnp.bfloat16), axis)
    start = jnp.broadcast_to(jnp.asarray(identity, shard.dtype), shard.shape)

    def step(k, before):
        at = length - 1 - k if reverse else k
        reached = at > index if reverse else at < index
        new = combine(before, everything[at].astype(shard.dtype))
        return jnp.where(reached, new, before)

    return lax.fori_loop(0, length, step, start)


def shifted(block, axis, distance):
    devices = range(lax.axis_size(axis))
    route = [(i - distance, i) for i in devices if i - distance in devices]
    return lax.ppermute(block, axis, route)


def add_single(before_part, after_part):
    return before_part + after_part


def silu_grads(pre_gate, pre_up, hidden_grad):
    sigmoid_gate = jax.nn.sigmoid(pre_gate)
    gate_grad = hidden_grad * pre_up * sigmoid_gate * (1.0 + pre_gate * (1.0 - sigmoid_gate))
    up_grad = hidden_grad * pre_gate * sigmoid_gate
    return (gate_grad.astype(jnp.bfloat16), up_grad.astype(jnp.bfloat16))


def dot(a, b):
    return jnp.dot(a, b, preferred_element_type=F32)


def dot_t(a, b):
    return lax.dot_general(a, b, (((1,), (1,)), ((), ())), preferred_element_type=F32)


def arrived(ref, sem):
    pltpu.make_async_copy(ref, ref, sem).wait()


def send(src, dst, send_sem, recv_sem, device):
    copy = pltpu.make_async_remote_copy(
        src_ref=src,
        dst_ref=dst,
        send_sem=send_sem,
        recv_sem=recv_sem,
        device_id=device,
        device_id_type=MESH,
    )
    copy.start()
    return copy


def greet(axes):
    barrier = pltpu.get_barrier_semaphore()
    count = 0
    for axis in axes:
        size, me = lax.axis_size(axis), lax.axis_index(axis)
        for off in range(1, size):
            pl.semaphore_signal(
                barrier, inc=1, device_id={axis: lax.rem(me + off, size)}, device_id_type=MESH
            )
            count += 1
    pl.semaphore_wait(barrier, count)


def slots_of(ids_t, cap, expert_count):
    chosen, rows = ids_t.shape
    experts = lax.broadcasted_iota(jnp.int32, (expert_count, rows), 0)
    named = [(experts == ids_t[k : k + 1, :]).astype(F32) for k in range(chosen)]
    earlier = (
        lax.broadcasted_iota(jnp.int32, (rows, rows), 0)
        < lax.broadcasted_iota(jnp.int32, (rows, rows), 1)
    ).astype(BF16)
    rank = dot(sum(named).astype(BF16), earlier)
    first = experts.astype(F32) * cap + rank
    return [jnp.sum(n * first, axis=0, keepdims=True) for n in named]


def slots_of_rows(ids, cap, expert_count):
    rows, chosen = ids.shape
    experts = lax.broadcasted_iota(jnp.int32, (rows, expert_count), 1)
    named = [(experts == ids[:, k : k + 1]).astype(F32) for k in range(chosen)]
    earlier = (
        lax.broadcasted_iota(jnp.int32, (rows, rows), 0)
        > lax.broadcasted_iota(jnp.int32, (rows, rows), 1)
    ).astype(BF16)
    rank = dot(earlier, sum(named).astype(BF16))
    first = experts.astype(F32) * cap + rank
    return [jnp.sum(n * first, axis=1, keepdims=True) for n in named]


def moe_kernel(
    cap,
    tile,
    ids_ref,
    ids_t_ref,
    weight_ref,
    input_ref,
    upstream_ref,
    gate_hbm,
    up_hbm,
    down_hbm,
    resid_ref,
    slots,
    received,
    w_gate,
    w_up,
    w_down,
    part,
    rep_in,
    half,
    sub_in,
    grads,
    out,
    returned,
    w_sem,
    own_sem,
    in_send,
    in_recv,
    rep_send,
    rep_recv,
    sub_send,
    sub_recv,
    agx_send,
    agx_recv,
    agr_send,
    agr_recv,
    out_send,
    out_recv,
):
    seqs, subs, reps = lax.axis_size("seq"), lax.axis_size("sub"), lax.axis_size("rep")
    seq, sub, rep = lax.axis_index("seq"), lax.axis_index("sub"), lax.axis_index("rep")
    local_experts, features, hidden = gate_hbm.shape
    experts = local_experts * seqs
    half_rows = half.shape[2]
    piece_rows = half_rows // subs
    sent = []

    weight_copies = [
        pltpu.make_async_copy(gate_hbm, w_gate, w_sem.at[0]),
        pltpu.make_async_copy(up_hbm, w_up, w_sem.at[1]),
        pltpu.make_async_copy(down_hbm, w_down, w_sem.at[2]),
    ]
    for copy in weight_copies:
        copy.start()

    def slot_rows(owner, e):
        return pl.ds(pl.multiple_of((owner * local_experts + e) * cap, 16), cap)

    def source_rows(source):
        return pl.ds(pl.multiple_of(source * cap, 16), cap)

    def half_of(r):
        return pl.ds(pl.multiple_of(r * half_rows, 16), half_rows)

    def piece_of(s):
        return pl.ds(pl.multiple_of(s * piece_rows, 16), piece_rows)

    def rows_of(r, s):
        return pl.ds(pl.multiple_of(r * half_rows + s * piece_rows, 16), piece_rows)

    places = slots_of(ids_t_ref[...], cap, experts)
    slot_count = experts * cap
    slot_at = lax.broadcasted_iota(jnp.int32, (slot_count, places[0].shape[1]), 0).astype(F32)
    pick = jnp.zeros(slot_at.shape, F32)
    for place in places:
        pick = pick + (slot_at == place).astype(F32)
    pick = pick.astype(BF16)
    slots[:, :features] = dot(pick, input_ref[...]).astype(BF16)
    slots[:, features:] = dot(pick, upstream_ref[...]).astype(BF16)

    greet(("seq", "sub", "rep"))

    own = []
    for e in range(local_experts):
        copy = pltpu.make_async_copy(
            slots.at[slot_rows(seq, e)], received.at[e, source_rows(seq)], own_sem.at[e]
        )
        copy.start()
        own.append(copy)
        batch = []
        for off in range(1, seqs):
            target = lax.rem(seq + off, seqs)
            batch.append(
                send(
                    slots.at[slot_rows(target, e)],
                    received.at[e, source_rows(seq)],
                    in_send.at[e, off - 1],
                    in_recv.at[e, off - 1],
                    {"seq": target},
                )
            )
        if e < local_experts - 1:
            for copy in batch:
                copy.wait_send()
        else:
            sent.extend(batch)
    for copy in weight_copies:
        copy.wait()

    def first_products(e):
        own[e].wait()
        for off in range(1, seqs):
            source = lax.rem(seq + seqs - off, seqs)
            arrived(received.at[e, source_rows(source)], in_recv.at[e, off - 1])
        for a in range(3):

            @pl.loop(0, hidden // tile)
            def _(j):
                cols = pl.ds(pl.multiple_of(j * tile, tile), tile)
                if a == 0:
                    got = dot(received[e, :, :features], w_gate[e, :, cols])
                elif a == 1:
                    got = dot(received[e, :, :features], w_up[e, :, cols])
                else:
                    got = dot_t(received[e, :, features:], w_down[e, cols, :])
                part[e, a, :, cols] = got.astype(BF16)

            for off in range(1, reps):
                target = lax.rem(rep + off, reps)
                sent.append(
                    send(
                        part.at[e, a, half_of(target)],
                        rep_in.at[e, a, off - 1],
                        rep_send.at[e, a, off - 1],
                        rep_recv.at[e, a, off - 1],
                        {"rep": target},
                    )
                )
        for a in range(3):
            for off in range(1, reps):
                arrived(rep_in.at[e, a, off - 1], rep_recv.at[e, a, off - 1])
            total = part[e, a, half_of(rep), :].astype(F32)
            for off in range(1, reps):
                total = total + rep_in[e, a, off - 1].astype(F32)
            half[e, a] = total.astype(BF16)
            for off in range(1, subs):
                target = lax.rem(sub + off, subs)
                sent.append(
                    send(
                        half.at[e, a, piece_of(target)],
                        sub_in.at[e, a, off - 1],
                        sub_send.at[e, a, off - 1],
                        sub_recv.at[e, a, off - 1],
                        {"sub": target},
                    )
                )

    def gate(e):
        sums = []
        for a in range(3):
            for off in range(1, subs):
                arrived(sub_in.at[e, a, off - 1], sub_recv.at[e, a, off - 1])
            total = half[e, a, piece_of(sub), :].astype(F32)
            for off in range(1, subs):
                total = total + sub_in[e, a, off - 1].astype(F32)
            sums.append(total)
        gate_grad, up_grad = silu_grads(*sums)
        mine = rows_of(rep, sub)
        grads[e, mine, :hidden] = gate_grad
        grads[e, mine, hidden:] = up_grad
        for off in range(1, subs):
            target = lax.rem(sub + off, subs)
            sent.append(
                send(
                    grads.at[e, mine],
                    grads.at[e, mine],
                    agx_send.at[e, off - 1],
                    agx_recv.at[e, off - 1],
                    {"sub": target},
                )
            )
        pass_on(e, 0)

    def pass_on(e, sub_off):
        piece = rows_of(rep, lax.rem(sub + subs - sub_off, subs))
        for off in range(1, reps):
            target = lax.rem(rep + off, reps)
            sent.append(
                send(
                    grads.at[e, piece],
                    grads.at[e, piece],
                    agr_send.at[e, off - 1, sub_off],
                    agr_recv.at[e, off - 1, sub_off],
                    {"rep": target},
                )
            )

    def second_products(e):
        for sub_off in range(1, subs):
            arrived(
                grads.at[e, rows_of(rep, lax.rem(sub + subs - sub_off, subs))],
                agx_recv.at[e, sub_off - 1],
            )
            pass_on(e, sub_off)
        for off in range(1, reps):
            for sub_off in range(subs):
                piece = rows_of(
                    lax.rem(rep + reps - off, reps), lax.rem(sub + subs - sub_off, subs)
                )
                arrived(grads.at[e, piece], agr_recv.at[e, off - 1, sub_off])

        step = min(tile, features)

        @pl.loop(0, features // step)
        def _(j):
            cols = pl.ds(pl.multiple_of(j * step, step), step)
            got = dot_t(grads[e, :, :hidden], w_gate[e, cols, :])
            got = got + dot_t(grads[e, :, hidden:], w_up[e, cols, :])
            out[e, :, cols] = got.astype(BF16)

        copy = pltpu.make_async_copy(
            out.at[e, source_rows(seq)], returned.at[slot_rows(seq, e)], own_sem.at[e]
        )
        copy.start()
        own[e] = copy
        for off in range(1, seqs):
            target = lax.rem(seq + off, seqs)
            sent.append(
                send(
                    out.at[e, source_rows(target)],
                    returned.at[slot_rows(seq, e)],
                    out_send.at[e, off - 1],
                    out_recv.at[e, off - 1],
                    {"seq": target},
                )
            )

    for e in range(local_experts):
        first_products(e)
        if e > 0:
            second_products(e - 1)
        gate(e)
    second_products(local_experts - 1)

    places = slots_of_rows(ids_ref[...], cap, experts)
    rows = ids_ref.shape[0]
    slot_at = lax.broadcasted_iota(jnp.int32, (rows, slot_count), 1).astype(F32)
    for e in range(local_experts):
        own[e].wait()
        for off in range(1, seqs):
            source = lax.rem(seq + seqs - off, seqs)
            arrived(returned.at[slot_rows(source, e)], out_recv.at[e, off - 1])
    combined = upstream_ref[...].astype(F32)
    for k, place in enumerate(places):
        pick = (slot_at == place).astype(BF16)
        combined = combined + weight_ref[:, k : k + 1] * dot(pick, returned[...])
    resid_ref[...] = combined.astype(BF16)
    for copy in sent:
        copy.wait_send()


def moe_backward(moe_input, upstream, expert_ids, router_weight, w_gate, w_up, w_down):
    rows, features = moe_input.shape
    seqs, subs, reps = lax.axis_size("seq"), lax.axis_size("sub"), lax.axis_size("rep")
    local_experts, _, hidden = w_gate.shape
    experts = local_experts * seqs
    cap = max(2, 3 * rows // experts)
    cap = -(-cap // 16) * 16
    while seqs * cap % (16 * subs * reps):
        cap += 16
    tile = 256 if hidden % 256 == 0 else hidden
    block = seqs * cap
    half_rows = block // reps
    piece_rows = half_rows // subs
    vmem = pl.BlockSpec(memory_space=pltpu.VMEM)
    hbm = pl.BlockSpec(memory_space=pl.ANY)
    dma = pltpu.SemaphoreType.DMA
    n = local_experts
    return pl.pallas_call(
        functools.partial(moe_kernel, cap, tile),
        out_shape=jax.ShapeDtypeStruct((rows, features), BF16),
        in_specs=[vmem] * 5 + [hbm] * 3,
        out_specs=vmem,
        scratch_shapes=[
            pltpu.VMEM((experts * cap, 2 * features), BF16),
            pltpu.VMEM((n, block, 2 * features), BF16),
            pltpu.VMEM(w_gate.shape, BF16),
            pltpu.VMEM(w_up.shape, BF16),
            pltpu.VMEM(w_down.shape, BF16),
            pltpu.VMEM((n, 3, block, hidden), BF16),
            pltpu.VMEM((n, 3, reps - 1, half_rows, hidden), BF16),
            pltpu.VMEM((n, 3, half_rows, hidden), BF16),
            pltpu.VMEM((n, 3, subs - 1, piece_rows, hidden), BF16),
            pltpu.VMEM((n, block, 2 * hidden), BF16),
            pltpu.VMEM((n, block, features), BF16),
            pltpu.VMEM((experts * cap, features), BF16),
            dma((3,)),
            dma((n,)),
            dma((n, seqs - 1)),
            dma((n, seqs - 1)),
            dma((n, 3, reps - 1)),
            dma((n, 3, reps - 1)),
            dma((n, 3, subs - 1)),
            dma((n, 3, subs - 1)),
            dma((n, subs - 1)),
            dma((n, subs - 1)),
            dma((n, reps - 1, subs)),
            dma((n, reps - 1, subs)),
            dma((n, seqs - 1)),
            dma((n, seqs - 1)),
        ],
        compiler_params=pltpu.CompilerParams(
            collective_id=0, has_side_effects=True, vmem_limit_bytes=56 * 1024 * 1024
        ),
        name="experts",
    )(expert_ids, expert_ids.T, router_weight, moe_input, upstream, w_gate, w_up, w_down)


def window_block(query_heads, keys_ext, values_ext, grad_heads, first_key):
    row_count = query_heads.shape[0]
    key_count = keys_ext.shape[0]
    scaling = query_heads.shape[-1] ** (-0.5)
    query_pos = lax.broadcasted_iota(jnp.int32, (row_count, key_count), 0)
    key_pos = lax.broadcasted_iota(jnp.int32, (row_count, key_count), 1)
    allowed = (key_pos > query_pos) & (key_pos <= query_pos + WINDOW) & (key_pos + first_key >= 0)
    scores = (
        jnp.einsum("ihd,jhd->hij", query_heads, keys_ext, preferred_element_type=jnp.float32)
        * scaling
    )
    scores = jnp.where(allowed[None], scores, -jnp.inf)
    highest = jnp.max(scores, axis=2, keepdims=True)
    weights = jnp.exp(scores - highest)
    softmax_probs = weights / jnp.sum(weights, axis=2, keepdims=True)
    probs_low = softmax_probs.astype(jnp.bfloat16)
    attended = jnp.einsum("hij,jhe->ihe", probs_low, values_ext, preferred_element_type=jnp.float32)
    centre = jnp.sum(grad_heads.astype(jnp.float32) * attended, axis=2)
    prob_grad = jnp.einsum(
        "ihe,jhe->hij", grad_heads, values_ext, preferred_element_type=jnp.float32
    )
    score_grad = (softmax_probs * (prob_grad - jnp.transpose(centre)[:, :, None])).astype(
        jnp.bfloat16
    )
    win_query = (
        jnp.einsum("hij,jhd->ihd", score_grad, keys_ext, preferred_element_type=jnp.float32)
        * scaling
    )
    win_key = (
        jnp.einsum("hij,ihd->jhd", score_grad, query_heads, preferred_element_type=jnp.float32)
        * scaling
    )
    win_value = jnp.einsum(
        "hij,ihe->jhe", probs_low, grad_heads, preferred_element_type=jnp.float32
    )
    return (win_query, win_key, win_value)


def local(
    moe_input,
    upstream,
    expert_ids,
    router_weight,
    w_gate,
    w_up,
    w_down,
    out_proj,
    query,
    key_in,
    value,
):
    row_count, features = moe_input.shape
    seq_count = lax.axis_size("seq")
    resid_grad = moe_backward(
        moe_input, upstream, expert_ids, router_weight, w_gate, w_up, w_down
    )
    head_grad = lax.dot_general(
        lax.all_gather(resid_grad, ("sub", "rep"), axis=1, tiled=True),
        out_proj,
        (((1,), (1,)), ((), ())),
        preferred_element_type=jnp.float32,
    ).astype(jnp.bfloat16)
    head_dim = HEAD_DIM
    local_heads = features // head_dim
    head_shape = (row_count, local_heads, head_dim)
    query_heads = query.reshape(head_shape)
    key_heads = key_in.reshape(head_shape)
    value_heads = value.reshape(head_shape)
    grad_heads = head_grad.reshape(head_shape)
    state_local = jnp.einsum(
        "shd,she->hde", key_heads, value_heads, preferred_element_type=jnp.float32
    )
    grad_local = jnp.einsum(
        "shd,she->hde", query_heads, grad_heads, preferred_element_type=jnp.float32
    )
    zero_state = jnp.zeros_like(state_local)
    preceding_state = entering(state_local, "seq", add_single, zero_state, False)
    gradient_following = entering(grad_local, "seq", add_single, zero_state, True)
    causal_masking = (
        lax.broadcasted_iota(jnp.int32, (row_count, row_count), 0)
        >= lax.broadcasted_iota(jnp.int32, (row_count, row_count), 1)
    )[None]
    value_products = jnp.where(
        causal_masking,
        jnp.einsum("ihe,jhe->hij", grad_heads, value_heads, preferred_element_type=jnp.float32),
        0.0,
    ).astype(jnp.bfloat16)
    query_products = jnp.where(
        causal_masking,
        jnp.einsum("ihd,jhd->hij", query_heads, key_heads, preferred_element_type=jnp.float32),
        0.0,
    ).astype(jnp.bfloat16)
    linear_branch_scale = (head_dim * row_count * seq_count) ** (-0.5)
    exact_precision = lax.Precision.HIGHEST
    linear_query = linear_branch_scale * (
        jnp.einsum(
            "ihe,hde->ihd",
            grad_heads.astype(jnp.float32),
            preceding_state,
            precision=exact_precision,
        )
        + jnp.einsum("hij,jhd->ihd", value_products, key_heads, preferred_element_type=jnp.float32)
    )
    lin_key = linear_branch_scale * (
        jnp.einsum(
            "jhe,hde->jhd",
            value_heads.astype(jnp.float32),
            gradient_following,
            precision=exact_precision,
        )
        + jnp.einsum(
            "hij,ihd->jhd", value_products, query_heads, preferred_element_type=jnp.float32
        )
    )
    linear_value = linear_branch_scale * (
        jnp.einsum(
            "jhd,hde->jhe",
            key_heads.astype(jnp.float32),
            gradient_following,
            precision=exact_precision,
        )
        + jnp.einsum("hij,ihe->jhe", query_products, grad_heads, preferred_element_type=jnp.float32)
    )
    window = WINDOW
    first_row = lax.axis_index("seq") * row_count
    halo_keys, halo_values = shifted(
        (key_heads[row_count - window :], value_heads[row_count - window :]), "seq", 1
    )
    keys_ext = jnp.concatenate([halo_keys, key_heads], axis=0)
    values_ext = jnp.concatenate([halo_values, value_heads], axis=0)
    win_query, key_ext_grad, value_ext_grad = window_block(
        query_heads, keys_ext, values_ext, grad_heads, first_row - window
    )
    carried_key, carried_value = (
        shifted(key_ext_grad[:window].astype(jnp.bfloat16), "seq", -1).astype(jnp.float32),
        shifted(value_ext_grad[:window].astype(jnp.bfloat16), "seq", -1).astype(jnp.float32),
    )
    padding = jnp.zeros((row_count - window, local_heads, head_dim), jnp.float32)
    win_key = key_ext_grad[window:] + jnp.concatenate([padding, carried_key], axis=0)
    win_value = value_ext_grad[window:] + jnp.concatenate([padding, carried_value], axis=0)
    query_grad = (linear_query + win_query).astype(jnp.bfloat16).reshape(row_count, features)
    key_grad = (lin_key + win_key).astype(jnp.bfloat16).reshape(row_count, features)
    value_grad = (linear_value + win_value).astype(jnp.bfloat16).reshape(row_count, features)
    return (resid_grad, query_grad, key_grad, value_grad)


def solution(mesh):
    return jax.shard_map(
        local,
        mesh=mesh,
        in_specs=(
            P(("groups", "seq"), ("sub", "rep")),
            P(("groups", "seq"), ("sub", "rep")),
            P(("groups", "seq"), None),
            P(("groups", "seq"), None),
            P("seq", ("sub", "rep"), None),
            P("seq", ("sub", "rep"), None),
            P("seq", None, ("sub", "rep")),
            P(("sub", "rep"), None),
            P(("groups", "seq"), ("sub", "rep")),
            P(("groups", "seq"), ("sub", "rep")),
            P(("groups", "seq"), ("sub", "rep")),
        ),
        out_specs=(
            P(("groups", "seq"), ("sub", "rep")),
            P(("groups", "seq"), ("sub", "rep")),
            P(("groups", "seq"), ("sub", "rep")),
            P(("groups", "seq"), ("sub", "rep")),
        ),
        check_vma=False,
    )
```

```python
import functools

import jax
import jax.numpy as jnp
from jax import lax
from jax.experimental import pallas as pl
from jax.experimental.pallas import tpu as pltpu
from jax.sharding import PartitionSpec as P

HEAD_DIM = 128
WINDOW = 128
MESH = pl.DeviceIdType.MESH
F32 = jnp.float32
BF16 = jnp.bfloat16


def silu_grads(pre_gate, pre_up, hidden_grad):
    sigmoid_gate = jax.nn.sigmoid(pre_gate)
    gate_grad = hidden_grad * pre_up * sigmoid_gate * (1.0 + pre_gate * (1.0 - sigmoid_gate))
    up_grad = hidden_grad * pre_gate * sigmoid_gate
    return (gate_grad.astype(jnp.bfloat16), up_grad.astype(jnp.bfloat16))


def dot(a, b):
    return jnp.dot(a, b, preferred_element_type=F32)


def dot_t(a, b):
    return lax.dot_general(a, b, (((1,), (1,)), ((), ())), preferred_element_type=F32)


def arrived(ref, sem):
    pltpu.make_async_copy(ref, ref, sem).wait()


def send(src, dst, send_sem, recv_sem, device):
    copy = pltpu.make_async_remote_copy(
        src_ref=src,
        dst_ref=dst,
        send_sem=send_sem,
        recv_sem=recv_sem,
        device_id=device,
        device_id_type=MESH,
    )
    copy.start()
    return copy


def greet(axes):
    barrier = pltpu.get_barrier_semaphore()
    count = 0
    for axis in axes:
        size, me = lax.axis_size(axis), lax.axis_index(axis)
        for off in range(1, size):
            pl.semaphore_signal(
                barrier, inc=1, device_id={axis: lax.rem(me + off, size)}, device_id_type=MESH
            )
            count += 1
    pl.semaphore_wait(barrier, count)


def slots_of(ids_t, cap, expert_count):
    chosen, rows = ids_t.shape
    experts = lax.broadcasted_iota(jnp.int32, (expert_count, rows), 0)
    named = [(experts == ids_t[k : k + 1, :]).astype(F32) for k in range(chosen)]
    earlier = (
        lax.broadcasted_iota(jnp.int32, (rows, rows), 0)
        < lax.broadcasted_iota(jnp.int32, (rows, rows), 1)
    ).astype(BF16)
    rank = dot(sum(named).astype(BF16), earlier)
    first = experts.astype(F32) * cap + rank
    return [jnp.sum(n * first, axis=0, keepdims=True) for n in named]


def as_column(line):
    count = line.shape[1]
    same = lax.broadcasted_iota(jnp.int32, (count, count), 0) == lax.broadcasted_iota(
        jnp.int32, (count, count), 1
    )
    return jnp.sum(jnp.where(same, line, 0.0), axis=1, keepdims=True)


def dot_0(a, b):
    return lax.dot_general(a, b, (((0,), (0,)), ((), ())), preferred_element_type=F32)


def kernel(
    cap,
    tile,
    ids_ref,
    weight_ref,
    input_ref,
    upstream_ref,
    query_ref,
    key_ref,
    value_ref,
    gate_hbm,
    up_hbm,
    down_hbm,
    proj_hbm,
    resid_ref,
    query_grad_ref,
    key_grad_ref,
    value_grad_ref,
    slots,
    received,
    w_gate,
    w_up,
    w_down,
    part,
    rep_in,
    half,
    sub_in,
    grads,
    out,
    returned,
    proj,
    keys_ext,
    values_ext,
    probs,
    attended,
    query_dots,
    state,
    state_in,
    before,
    grad_state,
    grad_state_in,
    after,
    full,
    head_grad,
    query_sum,
    key_sum,
    value_sum,
    carry,
    carry_in,
    w_sem,
    own_sem,
    in_send,
    in_recv,
    rep_send,
    rep_recv,
    sub_send,
    sub_recv,
    agx_send,
    agx_recv,
    agr_send,
    agr_recv,
    out_send,
    out_recv,
    halo_send,
    halo_recv,
    state_send,
    state_recv,
    after_send,
    after_recv,
    resx_send,
    resx_recv,
    resr_send,
    resr_recv,
    carry_send,
    carry_recv,
):
    seqs, subs, reps = lax.axis_size("seq"), lax.axis_size("sub"), lax.axis_size("rep")
    seq, sub, rep = lax.axis_index("seq"), lax.axis_index("sub"), lax.axis_index("rep")
    local_experts, features, hidden = gate_hbm.shape
    experts = local_experts * seqs
    half_rows = half.shape[2]
    piece_rows = half_rows // subs
    sent = []
    sent_if = []
    rows = ids_ref.shape[1]
    heads = features // HEAD_DIM
    window = WINDOW
    pieces = subs * reps

    def send_if(cond, src, dst, send_sem, recv_sem, device):
        copy = pltpu.make_async_remote_copy(
            src_ref=src,
            dst_ref=dst,
            send_sem=send_sem,
            recv_sem=recv_sem,
            device_id=device,
            device_id_type=MESH,
        )
        pl.when(cond)(copy.start)
        sent_if.append((cond, copy))

    def of_head(h):
        return pl.ds(h * HEAD_DIM, HEAD_DIM)

    weight_copies = [
        pltpu.make_async_copy(gate_hbm, w_gate, w_sem.at[0]),
        pltpu.make_async_copy(up_hbm, w_up, w_sem.at[1]),
        pltpu.make_async_copy(down_hbm, w_down, w_sem.at[2]),
        pltpu.make_async_copy(proj_hbm, proj, w_sem.at[3]),
    ]
    for copy in weight_copies:
        copy.start()

    def slot_rows(owner, e):
        return pl.ds(pl.multiple_of((owner * local_experts + e) * cap, 16), cap)

    def source_rows(source):
        return pl.ds(pl.multiple_of(source * cap, 16), cap)

    def half_of(r):
        return pl.ds(pl.multiple_of(r * half_rows, 16), half_rows)

    def piece_of(s):
        return pl.ds(pl.multiple_of(s * piece_rows, 16), piece_rows)

    def rows_of(r, s):
        return pl.ds(pl.multiple_of(r * half_rows + s * piece_rows, 16), piece_rows)

    places = slots_of(ids_ref[...], cap, experts)
    slot_count = experts * cap
    slot_at = lax.broadcasted_iota(jnp.int32, (slot_count, places[0].shape[1]), 0).astype(F32)
    pick = jnp.zeros(slot_at.shape, F32)
    for place in places:
        pick = pick + (slot_at == place).astype(F32)
    pick = pick.astype(BF16)
    slots[:, :features] = dot(pick, input_ref[...]).astype(BF16)
    slots[:, features:] = dot(pick, upstream_ref[...]).astype(BF16)

    greet(("seq", "sub", "rep"))

    own = []
    for e in range(local_experts):
        copy = pltpu.make_async_copy(
            slots.at[slot_rows(seq, e)], received.at[e, source_rows(seq)], own_sem.at[e]
        )
        copy.start()
        own.append(copy)
        batch = []
        for off in range(1, seqs):
            target = lax.rem(seq + off, seqs)
            batch.append(
                send(
                    slots.at[slot_rows(target, e)],
                    received.at[e, source_rows(seq)],
                    in_send.at[e, off - 1],
                    in_recv.at[e, off - 1],
                    {"seq": target},
                )
            )
        if e < local_experts - 1:
            for copy in batch:
                copy.wait_send()
        else:
            sent.extend(batch)
    for copy in weight_copies:
        copy.wait()

    def first_products(e):
        own[e].wait()
        for off in range(1, seqs):
            source = lax.rem(seq + seqs - off, seqs)
            arrived(received.at[e, source_rows(source)], in_recv.at[e, off - 1])
        for a in range(3):

            @pl.loop(0, hidden // tile)
            def _(j):
                cols = pl.ds(pl.multiple_of(j * tile, tile), tile)
                if a == 0:
                    got = dot(received[e, :, :features], w_gate[e, :, cols])
                elif a == 1:
                    got = dot(received[e, :, :features], w_up[e, :, cols])
                else:
                    got = dot_t(received[e, :, features:], w_down[e, cols, :])
                part[e, a, :, cols] = got.astype(BF16)

            for off in range(1, reps):
                target = lax.rem(rep + off, reps)
                sent.append(
                    send(
                        part.at[e, a, half_of(target)],
                        rep_in.at[e, a, off - 1],
                        rep_send.at[e, a, off - 1],
                        rep_recv.at[e, a, off - 1],
                        {"rep": target},
                    )
                )
        for a in range(3):
            for off in range(1, reps):
                arrived(rep_in.at[e, a, off - 1], rep_recv.at[e, a, off - 1])
            total = part[e, a, half_of(rep), :].astype(F32)
            for off in range(1, reps):
                total = total + rep_in[e, a, off - 1].astype(F32)
            half[e, a] = total.astype(BF16)
            for off in range(1, subs):
                target = lax.rem(sub + off, subs)
                sent.append(
                    send(
                        half.at[e, a, piece_of(target)],
                        sub_in.at[e, a, off - 1],
                        sub_send.at[e, a, off - 1],
                        sub_recv.at[e, a, off - 1],
                        {"sub": target},
                    )
                )

    def gate(e):
        sums = []
        for a in range(3):
            for off in range(1, subs):
                arrived(sub_in.at[e, a, off - 1], sub_recv.at[e, a, off - 1])
            total = half[e, a, piece_of(sub), :].astype(F32)
            for off in range(1, subs):
                total = total + sub_in[e, a, off - 1].astype(F32)
            sums.append(total)
        gate_grad, up_grad = silu_grads(*sums)
        mine = rows_of(rep, sub)
        grads[e, mine, :hidden] = gate_grad
        grads[e, mine, hidden:] = up_grad
        for off in range(1, subs):
            target = lax.rem(sub + off, subs)
            sent.append(
                send(
                    grads.at[e, mine],
                    grads.at[e, mine],
                    agx_send.at[e, off - 1],
                    agx_recv.at[e, off - 1],
                    {"sub": target},
                )
            )
        pass_on(e, 0)

    def pass_on(e, sub_off):
        piece = rows_of(rep, lax.rem(sub + subs - sub_off, subs))
        for off in range(1, reps):
            target = lax.rem(rep + off, reps)
            sent.append(
                send(
                    grads.at[e, piece],
                    grads.at[e, piece],
                    agr_send.at[e, off - 1, sub_off],
                    agr_recv.at[e, off - 1, sub_off],
                    {"rep": target},
                )
            )

    def second_products(e):
        for sub_off in range(1, subs):
            arrived(
                grads.at[e, rows_of(rep, lax.rem(sub + subs - sub_off, subs))],
                agx_recv.at[e, sub_off - 1],
            )
            pass_on(e, sub_off)
        for off in range(1, reps):
            for sub_off in range(subs):
                piece = rows_of(
                    lax.rem(rep + reps - off, reps), lax.rem(sub + subs - sub_off, subs)
                )
                arrived(grads.at[e, piece], agr_recv.at[e, off - 1, sub_off])

        step = min(tile, features)

        @pl.loop(0, features // step)
        def _(j):
            cols = pl.ds(pl.multiple_of(j * step, step), step)
            got = dot_t(grads[e, :, :hidden], w_gate[e, cols, :])
            got = got + dot_t(grads[e, :, hidden:], w_up[e, cols, :])
            out[e, :, cols] = got.astype(BF16)

        copy = pltpu.make_async_copy(
            out.at[e, source_rows(seq)], returned.at[slot_rows(seq, e)], own_sem.at[e]
        )
        copy.start()
        own[e] = copy
        for off in range(1, seqs):
            target = lax.rem(seq + off, seqs)
            sent.append(
                send(
                    out.at[e, source_rows(target)],
                    returned.at[slot_rows(seq, e)],
                    out_send.at[e, off - 1],
                    out_recv.at[e, off - 1],
                    {"seq": target},
                )
            )

    def own_parts():
        keys_ext[window:, :] = key_ref[...]
        values_ext[window:, :] = value_ref[...]

        @pl.when(seq == 0)
        def _():
            keys_ext[:window, :] = jnp.zeros((window, features), BF16)
            values_ext[:window, :] = jnp.zeros((window, features), BF16)

        @pl.when(seq == seqs - 1)
        def _():
            carry_in[...] = jnp.zeros(carry_in.shape, BF16)

        causal = lax.broadcasted_iota(jnp.int32, (rows, rows), 0) >= lax.broadcasted_iota(
            jnp.int32, (rows, rows), 1
        )
        for h in range(heads):
            cols = of_head(h)
            q, k, v = query_ref[:, cols], key_ref[:, cols], value_ref[:, cols]
            state[h] = dot_0(k, v).astype(BF16)
            query_dots[h] = jnp.where(causal, dot_t(q, k), 0.0).astype(BF16)
        before[...] = jnp.zeros(before.shape, F32)
        after[...] = jnp.zeros(after.shape, F32)

    def send_own_parts():
        tail = pl.ds(rows - window, window)
        for n, (src, dst) in enumerate(((key_ref, keys_ext), (value_ref, values_ext))):
            send_if(
                seq < seqs - 1,
                src.at[tail],
                dst.at[pl.ds(0, window)],
                halo_send.at[n],
                halo_recv.at[n],
                {"seq": lax.rem(seq + 1, seqs)},
            )
        for off in range(1, seqs):
            send_if(
                seq + off < seqs,
                state,
                state_in.at[off - 1],
                state_send.at[off - 1],
                state_recv.at[off - 1],
                {"seq": lax.rem(seq + off, seqs)},
            )

    def window_probs():
        @pl.when(seq > 0)
        def _():
            for n, dst in enumerate((keys_ext, values_ext)):
                arrived(dst.at[pl.ds(0, window)], halo_recv.at[n])

        shape = (rows, rows + window)
        query_pos = lax.broadcasted_iota(jnp.int32, shape, 0)
        key_pos = lax.broadcasted_iota(jnp.int32, shape, 1)
        allowed = (
            (key_pos > query_pos)
            & (key_pos <= query_pos + window)
            & (key_pos + (seq * rows - window) >= 0)
        )
        for h in range(heads):
            cols = of_head(h)
            scores = dot_t(query_ref[:, cols], keys_ext[:, cols]) * (HEAD_DIM**-0.5)
            scores = jnp.where(allowed, scores, -jnp.inf)
            weights = jnp.exp(scores - jnp.max(scores, axis=1, keepdims=True))
            softmax = weights / jnp.sum(weights, axis=1, keepdims=True)
            probs[h] = softmax
            attended[:, cols] = dot(softmax.astype(BF16), values_ext[:, cols])

    def states_before():
        for off in range(1, seqs):

            @pl.when(seq >= off)
            def _():
                arrived(state_in.at[off - 1], state_recv.at[off - 1])
                before[...] = before[...] + state_in[off - 1].astype(F32)

    own_parts()
    for e in range(local_experts):
        first_products(e)
        if e == local_experts - 1:
            send_own_parts()
        if e > 0:
            second_products(e - 1)
        if e == local_experts - 1:
            window_probs()
            states_before()
        gate(e)
    second_products(local_experts - 1)

    columns = [as_column(place) for place in places]
    pair_weights = [as_column(weight_ref[k : k + 1, :]) for k in range(len(places))]
    slot_at = lax.broadcasted_iota(jnp.int32, (rows, slot_count), 1).astype(F32)
    picks = [(slot_at == column).astype(BF16) for column in columns]
    for e in range(local_experts):
        own[e].wait()
        for off in range(1, seqs):
            source = lax.rem(seq + seqs - off, seqs)
            arrived(returned.at[slot_rows(source, e)], out_recv.at[e, off - 1])
    combined = upstream_ref[...].astype(F32)
    for pair_weight, pick in zip(pair_weights, picks):
        combined = combined + pair_weight * dot(pick, returned[...])
    resid = combined.astype(BF16)
    resid_ref[...] = resid

    def index_of(s, r):
        return s * reps + r

    def resid_on(sub_off):
        piece = index_of(lax.rem(sub + subs - sub_off, subs), rep)
        for off in range(1, reps):
            sent.append(
                send(
                    full.at[piece],
                    full.at[piece],
                    resr_send.at[off - 1, sub_off],
                    resr_recv.at[off - 1, sub_off],
                    {"rep": lax.rem(rep + off, reps)},
                )
            )

    def project(piece):
        cols = pl.ds(pl.multiple_of(piece * features, 128), features)
        return dot_t(full[piece], proj[:, cols])

    mine = index_of(sub, rep)
    full[mine] = resid
    for off in range(1, subs):
        sent.append(
            send(
                full.at[mine],
                full.at[mine],
                resx_send.at[off - 1],
                resx_recv.at[off - 1],
                {"sub": lax.rem(sub + off, subs)},
            )
        )
    resid_on(0)
    total = project(mine)
    for sub_off in range(subs):
        from_sub = lax.rem(sub + subs - sub_off, subs)
        if sub_off > 0:
            piece = index_of(from_sub, rep)
            arrived(full.at[piece], resx_recv.at[sub_off - 1])
            resid_on(sub_off)
            total = total + project(piece)
        for off in range(1, reps):
            piece = index_of(from_sub, lax.rem(rep + reps - off, reps))
            arrived(full.at[piece], resr_recv.at[off - 1, sub_off])
            total = total + project(piece)
    head_grad[...] = total.astype(BF16)

    for h in range(heads):
        cols = of_head(h)
        grad_state[h] = dot_0(query_ref[:, cols], head_grad[:, cols]).astype(BF16)
    for off in range(1, seqs):
        send_if(
            seq >= off,
            grad_state,
            grad_state_in.at[off - 1],
            after_send.at[off - 1],
            after_recv.at[off - 1],
            {"seq": lax.rem(seq + seqs - off, seqs)},
        )

    scaling = HEAD_DIM**-0.5
    for h in range(heads):
        cols = of_head(h)
        q, o = query_ref[:, cols], head_grad[:, cols]
        keys, values = keys_ext[:, cols], values_ext[:, cols]
        softmax = probs[h]
        centre = jnp.sum(o.astype(F32) * attended[:, cols], axis=1, keepdims=True)
        score_grad = (softmax * (dot_t(o, values) - centre)).astype(BF16)
        query_sum[:, cols] = dot(score_grad, keys) * scaling
        key_ext = dot_0(score_grad, q) * scaling
        value_ext = dot_0(softmax.astype(BF16), o)
        key_sum[:, cols] = key_ext[window:]
        value_sum[:, cols] = value_ext[window:]
        carry[0, :, cols] = key_ext[:window].astype(BF16)
        carry[1, :, cols] = value_ext[:window].astype(BF16)
    send_if(
        seq > 0,
        carry,
        carry_in,
        carry_send.at[0],
        carry_recv.at[0],
        {"seq": lax.rem(seq + seqs - 1, seqs)},
    )

    linear = float(HEAD_DIM * rows * seqs) ** -0.5
    causal = lax.broadcasted_iota(jnp.int32, (rows, rows), 0) >= lax.broadcasted_iota(
        jnp.int32, (rows, rows), 1
    )
    for h in range(heads):
        cols = of_head(h)
        q, k, v, o = query_ref[:, cols], key_ref[:, cols], value_ref[:, cols], head_grad[:, cols]
        value_dots = jnp.where(causal, dot_t(o, v), 0.0).astype(BF16)
        lin_query = dot(value_dots, k) + dot_t(o, before[h].astype(BF16))
        query_grad_ref[:, cols] = (query_sum[:, cols] + linear * lin_query).astype(BF16)
        key_sum[:, cols] = key_sum[:, cols] + linear * dot_0(value_dots, q)
        value_sum[:, cols] = value_sum[:, cols] + linear * dot_0(query_dots[h], o)

    for off in range(1, seqs):

        @pl.when(seq + off < seqs)
        def _():
            arrived(grad_state_in.at[off - 1], after_recv.at[off - 1])
            after[...] = after[...] + grad_state_in[off - 1].astype(F32)

    @pl.when(seq < seqs - 1)
    def _():
        arrived(carry_in, carry_recv.at[0])

    for h in range(heads):
        cols = of_head(h)
        k, v = key_ref[:, cols], value_ref[:, cols]
        later = after[h].astype(BF16)
        key_total = key_sum[:, cols] + linear * dot_t(v, later)
        value_total = value_sum[:, cols] + linear * dot(k, later)
        low = rows - window
        key_grad_ref[:low, cols] = key_total[:low].astype(BF16)
        value_grad_ref[:low, cols] = value_total[:low].astype(BF16)
        key_grad_ref[low:, cols] = (key_total[low:] + carry_in[0, :, cols].astype(F32)).astype(BF16)
        value_grad_ref[low:, cols] = (
            value_total[low:] + carry_in[1, :, cols].astype(F32)
        ).astype(BF16)
    for copy in sent:
        copy.wait_send()
    for cond, copy in sent_if:
        pl.when(cond)(copy.wait_send)


def local(
    moe_input,
    upstream,
    expert_ids,
    router_weight,
    w_gate,
    w_up,
    w_down,
    out_proj,
    query,
    key_in,
    value,
):
    rows, features = moe_input.shape
    seqs, subs, reps = lax.axis_size("seq"), lax.axis_size("sub"), lax.axis_size("rep")
    local_experts, _, hidden = w_gate.shape
    experts = local_experts * seqs
    cap = max(2, 3 * rows // experts)
    cap = -(-cap // 16) * 16
    while seqs * cap % (16 * subs * reps):
        cap += 16
    tile = 256 if hidden % 256 == 0 else hidden
    block = seqs * cap
    half_rows = block // reps
    piece_rows = half_rows // subs
    vmem = pl.BlockSpec(memory_space=pltpu.VMEM)
    hbm = pl.BlockSpec(memory_space=pl.ANY)
    dma = pltpu.SemaphoreType.DMA
    n = local_experts
    heads = features // HEAD_DIM
    states = (heads, HEAD_DIM, HEAD_DIM)
    return pl.pallas_call(
        functools.partial(kernel, cap, tile),
        out_shape=[jax.ShapeDtypeStruct((rows, features), BF16)] * 4,
        in_specs=[vmem] * 7 + [hbm] * 4,
        out_specs=[vmem] * 4,
        scratch_shapes=[
            pltpu.VMEM((experts * cap, 2 * features), BF16),
            pltpu.VMEM((n, block, 2 * features), BF16),
            pltpu.VMEM(w_gate.shape, BF16),
            pltpu.VMEM(w_up.shape, BF16),
            pltpu.VMEM(w_down.shape, BF16),
            pltpu.VMEM((n, 3, block, hidden), BF16),
            pltpu.VMEM((n, 3, reps - 1, half_rows, hidden), BF16),
            pltpu.VMEM((n, 3, half_rows, hidden), BF16),
            pltpu.VMEM((n, 3, subs - 1, piece_rows, hidden), BF16),
            pltpu.VMEM((n, block, 2 * hidden), BF16),
            pltpu.VMEM((n, block, features), BF16),
            pltpu.VMEM((experts * cap, features), BF16),
            pltpu.VMEM(out_proj.shape, BF16),
            pltpu.VMEM((rows + WINDOW, features), BF16),
            pltpu.VMEM((rows + WINDOW, features), BF16),
            pltpu.VMEM((heads, rows, rows + WINDOW), F32),
            pltpu.VMEM((rows, features), F32),
            pltpu.VMEM((heads, rows, rows), BF16),
            pltpu.VMEM(states, BF16),
            pltpu.VMEM((seqs - 1,) + states, BF16),
            pltpu.VMEM(states, F32),
            pltpu.VMEM(states, BF16),
            pltpu.VMEM((seqs - 1,) + states, BF16),
            pltpu.VMEM(states, F32),
            pltpu.VMEM((subs * reps, rows, features), BF16),
            pltpu.VMEM((rows, features), BF16),
            pltpu.VMEM((rows, features), F32),
            pltpu.VMEM((rows, features), F32),
            pltpu.VMEM((rows, features), F32),
            pltpu.VMEM((2, WINDOW, features), BF16),
            pltpu.VMEM((2, WINDOW, features), BF16),
            dma((4,)),
            dma((n,)),
            dma((n, seqs - 1)),
            dma((n, seqs - 1)),
            dma((n, 3, reps - 1)),
            dma((n, 3, reps - 1)),
            dma((n, 3, subs - 1)),
            dma((n, 3, subs - 1)),
            dma((n, subs - 1)),
            dma((n, subs - 1)),
            dma((n, reps - 1, subs)),
            dma((n, reps - 1, subs)),
            dma((n, seqs - 1)),
            dma((n, seqs - 1)),
            dma((2,)),
            dma((2,)),
            dma((seqs - 1,)),
            dma((seqs - 1,)),
            dma((seqs - 1,)),
            dma((seqs - 1,)),
            dma((subs - 1,)),
            dma((subs - 1,)),
            dma((reps - 1, subs)),
            dma((reps - 1, subs)),
            dma((1,)),
            dma((1,)),
        ],
        compiler_params=pltpu.CompilerParams(
            collective_id=0, has_side_effects=True, vmem_limit_bytes=56 * 1024 * 1024
        ),
        name="backward",
    )(
        expert_ids.T,
        router_weight.T,
        moe_input,
        upstream,
        query,
        key_in,
        value,
        w_gate,
        w_up,
        w_down,
        out_proj,
    )


def solution(mesh):
    return jax.shard_map(
        local,
        mesh=mesh,
        in_specs=(
            P(("groups", "seq"), ("sub", "rep")),
            P(("groups", "seq"), ("sub", "rep")),
            P(("groups", "seq"), None),
            P(("groups", "seq"), None),
            P("seq", ("sub", "rep"), None),
            P("seq", ("sub", "rep"), None),
            P("seq", None, ("sub", "rep")),
            P(("sub", "rep"), None),
            P(("groups", "seq"), ("sub", "rep")),
            P(("groups", "seq"), ("sub", "rep")),
            P(("groups", "seq"), ("sub", "rep")),
        ),
        out_specs=(
            P(("groups", "seq"), ("sub", "rep")),
            P(("groups", "seq"), ("sub", "rep")),
            P(("groups", "seq"), ("sub", "rep")),
            P(("groups", "seq"), ("sub", "rep")),
        ),
        check_vma=False,
    )
```

```python
import functools

import jax
import jax.numpy as jnp
from jax import lax
from jax.experimental import pallas as pl
from jax.experimental.pallas import tpu as pltpu
from jax.sharding import PartitionSpec as P

HEAD_DIM = 128
WINDOW = 128
SPLITS = 2
MESH = pl.DeviceIdType.MESH
F32 = jnp.float32
BF16 = jnp.bfloat16


def silu_grads(pre_gate, pre_up, hidden_grad):
    sigmoid_gate = jax.nn.sigmoid(pre_gate)
    gate_grad = hidden_grad * pre_up * sigmoid_gate * (1.0 + pre_gate * (1.0 - sigmoid_gate))
    up_grad = hidden_grad * pre_gate * sigmoid_gate
    return (gate_grad.astype(jnp.bfloat16), up_grad.astype(jnp.bfloat16))


def dot(a, b):
    return jnp.dot(a, b, preferred_element_type=F32)


def dot_t(a, b):
    return lax.dot_general(a, b, (((1,), (1,)), ((), ())), preferred_element_type=F32)


def arrived(ref, sem):
    pltpu.make_async_copy(ref, ref, sem).wait()


def send(src, dst, send_sem, recv_sem, device):
    copy = pltpu.make_async_remote_copy(
        src_ref=src,
        dst_ref=dst,
        send_sem=send_sem,
        recv_sem=recv_sem,
        device_id=device,
        device_id_type=MESH,
    )
    copy.start()
    return copy


def greet(axes):
    barrier = pltpu.get_barrier_semaphore()
    count = 0
    for axis in axes:
        size, me = lax.axis_size(axis), lax.axis_index(axis)
        for off in range(1, size):
            pl.semaphore_signal(
                barrier, inc=1, device_id={axis: lax.rem(me + off, size)}, device_id_type=MESH
            )
            count += 1
    pl.semaphore_wait(barrier, count)


def slots_of(ids, local_experts, splits, chunk_cap, seqs):
    chosen, rows = ids.shape
    block = seqs * chunk_cap
    experts = lax.broadcasted_iota(jnp.int32, (local_experts * seqs, rows), 0)
    named = [(experts == ids[k : k + 1, :]).astype(F32) for k in range(chosen)]
    earlier = (
        lax.broadcasted_iota(jnp.int32, (rows, rows), 0)
        < lax.broadcasted_iota(jnp.int32, (rows, rows), 1)
    ).astype(BF16)
    rank = dot(sum(named).astype(BF16), earlier)
    owner = jnp.zeros(experts.shape, F32)
    for i in range(1, seqs):
        owner = owner + (experts >= i * local_experts).astype(F32)
    local = experts.astype(F32) - owner * local_experts
    first = local * (splits * block) + owner * chunk_cap
    places = []
    for n in named:
        own_rank = jnp.sum(n * rank, axis=0, keepdims=True)
        place = jnp.sum(n * first, axis=0, keepdims=True) + own_rank
        for i in range(1, splits):
            place = place + (own_rank >= i * chunk_cap).astype(F32) * (block - chunk_cap)
        places.append(place)
    return places


def as_column(line):
    count = line.shape[1]
    same = lax.broadcasted_iota(jnp.int32, (count, count), 0) == lax.broadcasted_iota(
        jnp.int32, (count, count), 1
    )
    return jnp.sum(jnp.where(same, line, 0.0), axis=1, keepdims=True)


def dot_0(a, b):
    return lax.dot_general(a, b, (((0,), (0,)), ((), ())), preferred_element_type=F32)


def kernel(
    cap,
    splits,
    tile,
    ids_ref,
    weight_ref,
    input_ref,
    upstream_ref,
    query_ref,
    key_ref,
    value_ref,
    gate_hbm,
    up_hbm,
    down_hbm,
    proj_hbm,
    resid_ref,
    query_grad_ref,
    key_grad_ref,
    value_grad_ref,
    slots,
    received,
    w_gate,
    w_up,
    w_down,
    part,
    rep_in,
    half,
    sub_in,
    grads,
    out,
    returned,
    proj,
    keys_ext,
    values_ext,
    probs,
    attended,
    query_dots,
    state,
    state_in,
    before,
    grad_state,
    grad_state_in,
    after,
    full,
    head_grad,
    query_sum,
    key_sum,
    value_sum,
    carry,
    carry_in,
    w_sem,
    own_sem,
    in_send,
    in_recv,
    rep_send,
    rep_recv,
    sub_send,
    sub_recv,
    agx_send,
    agx_recv,
    agr_send,
    agr_recv,
    out_send,
    out_recv,
    halo_send,
    halo_recv,
    state_send,
    state_recv,
    after_send,
    after_recv,
    resx_send,
    resx_recv,
    resr_send,
    resr_recv,
    carry_send,
    carry_recv,
):
    seqs, subs, reps = lax.axis_size("seq"), lax.axis_size("sub"), lax.axis_size("rep")
    seq, sub, rep = lax.axis_index("seq"), lax.axis_index("sub"), lax.axis_index("rep")
    local_experts, features, hidden = gate_hbm.shape
    experts = local_experts * seqs
    half_rows = half.shape[2]
    piece_rows = half_rows // subs
    block = seqs * cap
    chunks = local_experts * splits
    sent = []
    sent_if = []
    rows = ids_ref.shape[1]
    heads = features // HEAD_DIM
    window = WINDOW
    pieces = subs * reps

    def send_if(cond, src, dst, send_sem, recv_sem, device):
        copy = pltpu.make_async_remote_copy(
            src_ref=src,
            dst_ref=dst,
            send_sem=send_sem,
            recv_sem=recv_sem,
            device_id=device,
            device_id_type=MESH,
        )
        pl.when(cond)(copy.start)
        sent_if.append((cond, copy))

    def of_head(h):
        return pl.ds(h * HEAD_DIM, HEAD_DIM)

    weight_copies = [
        pltpu.make_async_copy(gate_hbm, w_gate, w_sem.at[0]),
        pltpu.make_async_copy(up_hbm, w_up, w_sem.at[1]),
        pltpu.make_async_copy(down_hbm, w_down, w_sem.at[2]),
        pltpu.make_async_copy(proj_hbm, proj, w_sem.at[3]),
    ]
    for copy in weight_copies:
        copy.start()

    def slot_rows(owner, c):
        return pl.ds(pl.multiple_of(c * block + owner * cap, 16), cap)

    def source_rows(source):
        return pl.ds(pl.multiple_of(source * cap, 16), cap)

    def half_of(r):
        return pl.ds(pl.multiple_of(r * half_rows, 16), half_rows)

    def piece_of(s):
        return pl.ds(pl.multiple_of(s * piece_rows, 16), piece_rows)

    def rows_of(r, s):
        return pl.ds(pl.multiple_of(r * half_rows + s * piece_rows, 16), piece_rows)

    places = slots_of(ids_ref[...], local_experts, splits, cap, seqs)

    def fill(c):
        slot_at = lax.broadcasted_iota(jnp.int32, (block, rows), 0).astype(F32) + float(c * block)
        pick = jnp.zeros(slot_at.shape, F32)
        for place in places:
            pick = pick + (slot_at == place).astype(F32)
        pick = pick.astype(BF16)
        slots[c * block : (c + 1) * block, :features] = dot(pick, input_ref[...]).astype(BF16)
        slots[c * block : (c + 1) * block, features:] = dot(pick, upstream_ref[...]).astype(BF16)

    own = [None] * chunks
    batches = [None] * chunks

    def start(c):
        own[c] = pltpu.make_async_copy(
            slots.at[slot_rows(seq, c)], received.at[c, source_rows(seq)], own_sem.at[c]
        )
        own[c].start()
        batches[c] = []
        for off in range(1, seqs):
            target = lax.rem(seq + off, seqs)
            batches[c].append(
                send(
                    slots.at[slot_rows(target, c)],
                    received.at[c, source_rows(seq)],
                    in_send.at[c, off - 1],
                    in_recv.at[c, off - 1],
                    {"seq": target},
                )
            )

    def left(c):
        for copy in batches[c]:
            copy.wait_send()

    def first_products(e):
        own[e].wait()
        for off in range(1, seqs):
            source = lax.rem(seq + seqs - off, seqs)
            arrived(received.at[e, source_rows(source)], in_recv.at[e, off - 1])
        for a in range(3):

            @pl.loop(0, hidden // tile)
            def _(j):
                cols = pl.ds(pl.multiple_of(j * tile, tile), tile)
                if a == 0:
                    got = dot(received[e, :, :features], w_gate[e // splits, :, cols])
                elif a == 1:
                    got = dot(received[e, :, :features], w_up[e // splits, :, cols])
                else:
                    got = dot_t(received[e, :, features:], w_down[e // splits, cols, :])
                part[e, a, :, cols] = got.astype(BF16)

            for off in range(1, reps):
                target = lax.rem(rep + off, reps)
                sent.append(
                    send(
                        part.at[e, a, half_of(target)],
                        rep_in.at[e, a, off - 1],
                        rep_send.at[e, a, off - 1],
                        rep_recv.at[e, a, off - 1],
                        {"rep": target},
                    )
                )
        for a in range(3):
            for off in range(1, reps):
                arrived(rep_in.at[e, a, off - 1], rep_recv.at[e, a, off - 1])
            total = part[e, a, half_of(rep), :].astype(F32)
            for off in range(1, reps):
                total = total + rep_in[e, a, off - 1].astype(F32)
            half[e, a] = total.astype(BF16)
            for off in range(1, subs):
                target = lax.rem(sub + off, subs)
                sent.append(
                    send(
                        half.at[e, a, piece_of(target)],
                        sub_in.at[e, a, off - 1],
                        sub_send.at[e, a, off - 1],
                        sub_recv.at[e, a, off - 1],
                        {"sub": target},
                    )
                )

    def gate(e):
        sums = []
        for a in range(3):
            for off in range(1, subs):
                arrived(sub_in.at[e, a, off - 1], sub_recv.at[e, a, off - 1])
            total = half[e, a, piece_of(sub), :].astype(F32)
            for off in range(1, subs):
                total = total + sub_in[e, a, off - 1].astype(F32)
            sums.append(total)
        gate_grad, up_grad = silu_grads(*sums)
        mine = rows_of(rep, sub)
        grads[e, mine, :hidden] = gate_grad
        grads[e, mine, hidden:] = up_grad
        for off in range(1, subs):
            target = lax.rem(sub + off, subs)
            sent.append(
                send(
                    grads.at[e, mine],
                    grads.at[e, mine],
                    agx_send.at[e, off - 1],
                    agx_recv.at[e, off - 1],
                    {"sub": target},
                )
            )
        pass_on(e, 0)

    def pass_on(e, sub_off):
        piece = rows_of(rep, lax.rem(sub + subs - sub_off, subs))
        for off in range(1, reps):
            target = lax.rem(rep + off, reps)
            sent.append(
                send(
                    grads.at[e, piece],
                    grads.at[e, piece],
                    agr_send.at[e, off - 1, sub_off],
                    agr_recv.at[e, off - 1, sub_off],
                    {"rep": target},
                )
            )

    def second_products(e):
        for sub_off in range(1, subs):
            arrived(
                grads.at[e, rows_of(rep, lax.rem(sub + subs - sub_off, subs))],
                agx_recv.at[e, sub_off - 1],
            )
            pass_on(e, sub_off)
        for off in range(1, reps):
            for sub_off in range(subs):
                piece = rows_of(
                    lax.rem(rep + reps - off, reps), lax.rem(sub + subs - sub_off, subs)
                )
                arrived(grads.at[e, piece], agr_recv.at[e, off - 1, sub_off])

        step = min(tile, features)

        @pl.loop(0, features // step)
        def _(j):
            cols = pl.ds(pl.multiple_of(j * step, step), step)
            got = dot_t(grads[e, :, :hidden], w_gate[e // splits, cols, :])
            got = got + dot_t(grads[e, :, hidden:], w_up[e // splits, cols, :])
            out[e, :, cols] = got.astype(BF16)

        copy = pltpu.make_async_copy(
            out.at[e, source_rows(seq)], returned.at[slot_rows(seq, e)], own_sem.at[e]
        )
        copy.start()
        own[e] = copy
        for off in range(1, seqs):
            target = lax.rem(seq + off, seqs)
            sent.append(
                send(
                    out.at[e, source_rows(target)],
                    returned.at[slot_rows(seq, e)],
                    out_send.at[e, off - 1],
                    out_recv.at[e, off - 1],
                    {"seq": target},
                )
            )

    def own_parts():
        keys_ext[window:, :] = key_ref[...]
        values_ext[window:, :] = value_ref[...]

        @pl.when(seq == 0)
        def _():
            keys_ext[:window, :] = jnp.zeros((window, features), BF16)
            values_ext[:window, :] = jnp.zeros((window, features), BF16)

        @pl.when(seq == seqs - 1)
        def _():
            carry_in[...] = jnp.zeros(carry_in.shape, BF16)

        causal = lax.broadcasted_iota(jnp.int32, (rows, rows), 0) >= lax.broadcasted_iota(
            jnp.int32, (rows, rows), 1
        )
        for h in range(heads):
            cols = of_head(h)
            q, k, v = query_ref[:, cols], key_ref[:, cols], value_ref[:, cols]
            state[h] = dot_0(k, v).astype(BF16)
            query_dots[h] = jnp.where(causal, dot_t(q, k), 0.0).astype(BF16)
        before[...] = jnp.zeros(before.shape, F32)
        after[...] = jnp.zeros(after.shape, F32)

    def send_halos():
        tail = pl.ds(rows - window, window)
        for n, (src, dst) in enumerate(((key_ref, keys_ext), (value_ref, values_ext))):
            send_if(
                seq < seqs - 1,
                src.at[tail],
                dst.at[pl.ds(0, window)],
                halo_send.at[n],
                halo_recv.at[n],
                {"seq": lax.rem(seq + 1, seqs)},
            )

    def send_states():
        for off in range(1, seqs):
            send_if(
                seq + off < seqs,
                state,
                state_in.at[off - 1],
                state_send.at[off - 1],
                state_recv.at[off - 1],
                {"seq": lax.rem(seq + off, seqs)},
            )

    def window_probs():
        @pl.when(seq > 0)
        def _():
            for n, dst in enumerate((keys_ext, values_ext)):
                arrived(dst.at[pl.ds(0, window)], halo_recv.at[n])

        shape = (rows, rows + window)
        query_pos = lax.broadcasted_iota(jnp.int32, shape, 0)
        key_pos = lax.broadcasted_iota(jnp.int32, shape, 1)
        allowed = (
            (key_pos > query_pos)
            & (key_pos <= query_pos + window)
            & (key_pos + (seq * rows - window) >= 0)
        )
        for h in range(heads):
            cols = of_head(h)
            scores = dot_t(query_ref[:, cols], keys_ext[:, cols]) * (HEAD_DIM**-0.5)
            scores = jnp.where(allowed, scores, -jnp.inf)
            weights = jnp.exp(scores - jnp.max(scores, axis=1, keepdims=True))
            softmax = weights / jnp.sum(weights, axis=1, keepdims=True)
            probs[h] = softmax
            attended[:, cols] = dot(softmax.astype(BF16), values_ext[:, cols])

    def states_before():
        for off in range(1, seqs):

            @pl.when(seq >= off)
            def _():
                arrived(state_in.at[off - 1], state_recv.at[off - 1])
                before[...] = before[...] + state_in[off - 1].astype(F32)

    fill(0)
    greet(("seq", "sub", "rep"))
    start(0)
    for c in range(1, chunks):
        fill(c)
    own_parts()
    columns = [as_column(place) for place in places]
    pair_weights = [as_column(weight_ref[k : k + 1, :]) for k in range(len(places))]
    left(0)
    if chunks > 1:
        start(1)
    for copy in weight_copies:
        copy.wait()
    for c in range(chunks):
        first_products(c)
        if c + 1 < chunks:
            left(c + 1)
        if c + 2 < chunks:
            start(c + 2)
        if c == chunks - 1:
            send_halos()
        if c > 0:
            second_products(c - 1)
        gate(c)
    second_products(chunks - 1)
    window_probs()

    combined = upstream_ref[...].astype(F32)
    for c in range(chunks):
        slot_at = lax.broadcasted_iota(jnp.int32, (rows, block), 1).astype(F32) + float(c * block)
        own[c].wait()
        for off in range(1, seqs):
            source = lax.rem(seq + seqs - off, seqs)
            arrived(returned.at[slot_rows(source, c)], out_recv.at[c, off - 1])
        for pair_weight, column in zip(pair_weights, columns):
            pick = (slot_at == column).astype(BF16)
            combined = combined + pair_weight * dot(
                pick, returned[c * block : (c + 1) * block, :]
            )
    resid = combined.astype(BF16)
    resid_ref[...] = resid

    def index_of(s, r):
        return s * reps + r

    def resid_on(sub_off):
        piece = index_of(lax.rem(sub + subs - sub_off, subs), rep)
        for off in range(1, reps):
            sent.append(
                send(
                    full.at[piece],
                    full.at[piece],
                    resr_send.at[off - 1, sub_off],
                    resr_recv.at[off - 1, sub_off],
                    {"rep": lax.rem(rep + off, reps)},
                )
            )

    def project(piece):
        cols = pl.ds(pl.multiple_of(piece * features, 128), features)
        return dot_t(full[piece], proj[:, cols])

    mine = index_of(sub, rep)
    full[mine] = resid
    for off in range(1, subs):
        sent.append(
            send(
                full.at[mine],
                full.at[mine],
                resx_send.at[off - 1],
                resx_recv.at[off - 1],
                {"sub": lax.rem(sub + off, subs)},
            )
        )
    resid_on(0)
    send_states()
    total = project(mine)
    for sub_off in range(subs):
        from_sub = lax.rem(sub + subs - sub_off, subs)
        if sub_off > 0:
            piece = index_of(from_sub, rep)
            arrived(full.at[piece], resx_recv.at[sub_off - 1])
            resid_on(sub_off)
            total = total + project(piece)
        for off in range(1, reps):
            piece = index_of(from_sub, lax.rem(rep + reps - off, reps))
            arrived(full.at[piece], resr_recv.at[off - 1, sub_off])
            total = total + project(piece)
    head_grad[...] = total.astype(BF16)

    for h in range(heads):
        cols = of_head(h)
        grad_state[h] = dot_0(query_ref[:, cols], head_grad[:, cols]).astype(BF16)
    for off in range(1, seqs):
        send_if(
            seq >= off,
            grad_state,
            grad_state_in.at[off - 1],
            after_send.at[off - 1],
            after_recv.at[off - 1],
            {"seq": lax.rem(seq + seqs - off, seqs)},
        )

    scaling = HEAD_DIM**-0.5
    for h in range(heads):
        cols = of_head(h)
        q, o = query_ref[:, cols], head_grad[:, cols]
        keys, values = keys_ext[:, cols], values_ext[:, cols]
        softmax = probs[h]
        centre = jnp.sum(o.astype(F32) * attended[:, cols], axis=1, keepdims=True)
        score_grad = (softmax * (dot_t(o, values) - centre)).astype(BF16)
        query_sum[:, cols] = dot(score_grad, keys) * scaling
        key_ext = dot_0(score_grad, q) * scaling
        value_ext = dot_0(softmax.astype(BF16), o)
        key_sum[:, cols] = key_ext[window:]
        value_sum[:, cols] = value_ext[window:]
        carry[0, :, cols] = key_ext[:window].astype(BF16)
        carry[1, :, cols] = value_ext[:window].astype(BF16)
    send_if(
        seq > 0,
        carry,
        carry_in,
        carry_send.at[0],
        carry_recv.at[0],
        {"seq": lax.rem(seq + seqs - 1, seqs)},
    )

    linear = float(HEAD_DIM * rows * seqs) ** -0.5
    causal = lax.broadcasted_iota(jnp.int32, (rows, rows), 0) >= lax.broadcasted_iota(
        jnp.int32, (rows, rows), 1
    )
    for h in range(heads):
        cols = of_head(h)
        q, k, v, o = query_ref[:, cols], key_ref[:, cols], value_ref[:, cols], head_grad[:, cols]
        value_dots = jnp.where(causal, dot_t(o, v), 0.0).astype(BF16)
        query_sum[:, cols] = query_sum[:, cols] + linear * dot(value_dots, k)
        key_sum[:, cols] = key_sum[:, cols] + linear * dot_0(value_dots, q)
        value_sum[:, cols] = value_sum[:, cols] + linear * dot_0(query_dots[h], o)

    states_before()
    for h in range(heads):
        cols = of_head(h)
        lin_query = dot_t(head_grad[:, cols], before[h].astype(BF16))
        query_grad_ref[:, cols] = (query_sum[:, cols] + linear * lin_query).astype(BF16)
    for off in range(1, seqs):

        @pl.when(seq + off < seqs)
        def _():
            arrived(grad_state_in.at[off - 1], after_recv.at[off - 1])
            after[...] = after[...] + grad_state_in[off - 1].astype(F32)

    @pl.when(seq < seqs - 1)
    def _():
        arrived(carry_in, carry_recv.at[0])

    for h in range(heads):
        cols = of_head(h)
        k, v = key_ref[:, cols], value_ref[:, cols]
        later = after[h].astype(BF16)
        key_total = key_sum[:, cols] + linear * dot_t(v, later)
        value_total = value_sum[:, cols] + linear * dot(k, later)
        low = rows - window
        key_grad_ref[:low, cols] = key_total[:low].astype(BF16)
        value_grad_ref[:low, cols] = value_total[:low].astype(BF16)
        key_grad_ref[low:, cols] = (key_total[low:] + carry_in[0, :, cols].astype(F32)).astype(BF16)
        value_grad_ref[low:, cols] = (
            value_total[low:] + carry_in[1, :, cols].astype(F32)
        ).astype(BF16)
    for copy in sent:
        copy.wait_send()
    for cond, copy in sent_if:
        pl.when(cond)(copy.wait_send)


def local(
    moe_input,
    upstream,
    expert_ids,
    router_weight,
    w_gate,
    w_up,
    w_down,
    out_proj,
    query,
    key_in,
    value,
):
    rows, features = moe_input.shape
    seqs, subs, reps = lax.axis_size("seq"), lax.axis_size("sub"), lax.axis_size("rep")
    local_experts, _, hidden = w_gate.shape
    experts = local_experts * seqs
    cap = max(2, 3 * rows // experts)
    cap = -(-cap // 16) * 16
    while seqs * cap % (16 * subs * reps):
        cap += 16
    splits = SPLITS
    while cap % (16 * splits) or seqs * cap // splits % (16 * subs * reps):
        splits -= 1
    slot_count = experts * cap
    cap = cap // splits
    tile = 256 if hidden % 256 == 0 else hidden
    block = seqs * cap
    half_rows = block // reps
    piece_rows = half_rows // subs
    vmem = pl.BlockSpec(memory_space=pltpu.VMEM)
    hbm = pl.BlockSpec(memory_space=pl.ANY)
    dma = pltpu.SemaphoreType.DMA
    n = local_experts * splits
    heads = features // HEAD_DIM
    states = (heads, HEAD_DIM, HEAD_DIM)
    results = pl.pallas_call(
        functools.partial(kernel, cap, splits, tile),
        out_shape=[jax.ShapeDtypeStruct((rows, features), BF16)] * 4,
        in_specs=[vmem] * 7 + [hbm] * 4,
        out_specs=[vmem] * 4,
        scratch_shapes=[
            pltpu.VMEM((slot_count, 2 * features), BF16),
            pltpu.VMEM((n, block, 2 * features), BF16),
            pltpu.VMEM(w_gate.shape, BF16),
            pltpu.VMEM(w_up.shape, BF16),
            pltpu.VMEM(w_down.shape, BF16),
            pltpu.VMEM((n, 3, block, hidden), BF16),
            pltpu.VMEM((n, 3, reps - 1, half_rows, hidden), BF16),
            pltpu.VMEM((n, 3, half_rows, hidden), BF16),
            pltpu.VMEM((n, 3, subs - 1, piece_rows, hidden), BF16),
            pltpu.VMEM((n, block, 2 * hidden), BF16),
            pltpu.VMEM((n, block, features), BF16),
            pltpu.VMEM((slot_count, features), BF16),
            pltpu.VMEM(out_proj.shape, BF16),
            pltpu.VMEM((rows + WINDOW, features), BF16),
            pltpu.VMEM((rows + WINDOW, features), BF16),
            pltpu.VMEM((heads, rows, rows + WINDOW), F32),
            pltpu.VMEM((rows, features), F32),
            pltpu.VMEM((heads, rows, rows), BF16),
            pltpu.VMEM(states, BF16),
            pltpu.VMEM((seqs - 1,) + states, BF16),
            pltpu.VMEM(states, F32),
            pltpu.VMEM(states, BF16),
            pltpu.VMEM((seqs - 1,) + states, BF16),
            pltpu.VMEM(states, F32),
            pltpu.VMEM((subs * reps, rows, features), BF16),
            pltpu.VMEM((rows, features), BF16),
            pltpu.VMEM((rows, features), F32),
            pltpu.VMEM((rows, features), F32),
            pltpu.VMEM((rows, features), F32),
            pltpu.VMEM((2, WINDOW, features), BF16),
            pltpu.VMEM((2, WINDOW, features), BF16),
            dma((4,)),
            dma((n,)),
            dma((n, seqs - 1)),
            dma((n, seqs - 1)),
            dma((n, 3, reps - 1)),
            dma((n, 3, reps - 1)),
            dma((n, 3, subs - 1)),
            dma((n, 3, subs - 1)),
            dma((n, subs - 1)),
            dma((n, subs - 1)),
            dma((n, reps - 1, subs)),
            dma((n, reps - 1, subs)),
            dma((n, seqs - 1)),
            dma((n, seqs - 1)),
            dma((2,)),
            dma((2,)),
            dma((seqs - 1,)),
            dma((seqs - 1,)),
            dma((seqs - 1,)),
            dma((seqs - 1,)),
            dma((subs - 1,)),
            dma((subs - 1,)),
            dma((reps - 1, subs)),
            dma((reps - 1, subs)),
            dma((1,)),
            dma((1,)),
        ],
        compiler_params=pltpu.CompilerParams(
            collective_id=0, has_side_effects=True, vmem_limit_bytes=56 * 1024 * 1024
        ),
        name="backward",
    )(
        expert_ids.T,
        router_weight.T,
        moe_input,
        upstream,
        query,
        key_in,
        value,
        w_gate,
        w_up,
        w_down,
        out_proj,
    )
    return pl.pallas_call(
        place_kernel,
        out_shape=[jax.ShapeDtypeStruct((rows, features), BF16)] * 4,
        in_specs=[hbm] * 4,
        out_specs=[hbm] * 4,
        scratch_shapes=[dma((4,))],
        name="place",
    )(*results)


def place_kernel(*refs):
    sems = refs[-1]
    copies = [pltpu.make_async_copy(refs[i], refs[4 + i], sems.at[i]) for i in range(4)]
    for copy in copies:
        copy.start()
    for copy in copies:
        copy.wait()


def solution(mesh):
    return jax.shard_map(
        local,
        mesh=mesh,
        in_specs=(
            P(("groups", "seq"), ("sub", "rep")),
            P(("groups", "seq"), ("sub", "rep")),
            P(("groups", "seq"), None),
            P(("groups", "seq"), None),
            P("seq", ("sub", "rep"), None),
            P("seq", ("sub", "rep"), None),
            P("seq", None, ("sub", "rep")),
            P(("sub", "rep"), None),
            P(("groups", "seq"), ("sub", "rep")),
            P(("groups", "seq"), ("sub", "rep")),
            P(("groups", "seq"), ("sub", "rep")),
        ),
        out_specs=(
            P(("groups", "seq"), ("sub", "rep")),
            P(("groups", "seq"), ("sub", "rep")),
            P(("groups", "seq"), ("sub", "rep")),
            P(("groups", "seq"), ("sub", "rep")),
        ),
        check_vma=False,
    )
```

```python
import functools

import jax
import jax.numpy as jnp
from jax import lax
from jax.experimental import pallas as pl
from jax.experimental.pallas import tpu as pltpu
from jax.sharding import PartitionSpec as P

HEAD_DIM = 128
WINDOW = 128
SPLITS = 3
MESH = pl.DeviceIdType.MESH
F32 = jnp.float32
BF16 = jnp.bfloat16


def silu_grads(pre_gate, pre_up, hidden_grad):
    sigmoid_gate = jax.nn.sigmoid(pre_gate)
    gate_grad = hidden_grad * pre_up * sigmoid_gate * (1.0 + pre_gate * (1.0 - sigmoid_gate))
    up_grad = hidden_grad * pre_gate * sigmoid_gate
    return (gate_grad.astype(jnp.bfloat16), up_grad.astype(jnp.bfloat16))


def dot(a, b):
    return jnp.dot(a, b, preferred_element_type=F32)


def dot_t(a, b):
    return lax.dot_general(a, b, (((1,), (1,)), ((), ())), preferred_element_type=F32)


def arrived(ref, sem):
    pltpu.make_async_copy(ref, ref, sem).wait()


def send(src, dst, send_sem, recv_sem, device):
    copy = pltpu.make_async_remote_copy(
        src_ref=src,
        dst_ref=dst,
        send_sem=send_sem,
        recv_sem=recv_sem,
        device_id=device,
        device_id_type=MESH,
    )
    copy.start()
    return copy


def greet(axes):
    barrier = pltpu.get_barrier_semaphore()
    count = 0
    for axis in axes:
        size, me = lax.axis_size(axis), lax.axis_index(axis)
        for off in range(1, size):
            pl.semaphore_signal(
                barrier, inc=1, device_id={axis: lax.rem(me + off, size)}, device_id_type=MESH
            )
            count += 1
    pl.semaphore_wait(barrier, count)


def slots_of(ids, local_experts, splits, chunk_cap, seqs):
    chosen, rows = ids.shape
    block = seqs * chunk_cap
    experts = lax.broadcasted_iota(jnp.int32, (local_experts * seqs, rows), 0)
    named = [(experts == ids[k : k + 1, :]).astype(F32) for k in range(chosen)]
    earlier = (
        lax.broadcasted_iota(jnp.int32, (rows, rows), 0)
        < lax.broadcasted_iota(jnp.int32, (rows, rows), 1)
    ).astype(BF16)
    rank = dot(sum(named).astype(BF16), earlier)
    owner = jnp.zeros(experts.shape, F32)
    for i in range(1, seqs):
        owner = owner + (experts >= i * local_experts).astype(F32)
    local = experts.astype(F32) - owner * local_experts
    first = local * (splits * block) + owner * chunk_cap
    places = []
    for n in named:
        own_rank = jnp.sum(n * rank, axis=0, keepdims=True)
        place = jnp.sum(n * first, axis=0, keepdims=True) + own_rank
        for i in range(1, splits):
            place = place + (own_rank >= i * chunk_cap).astype(F32) * (block - chunk_cap)
        places.append(place)
    return places


def as_column(line):
    count = line.shape[1]
    same = lax.broadcasted_iota(jnp.int32, (count, count), 0) == lax.broadcasted_iota(
        jnp.int32, (count, count), 1
    )
    return jnp.sum(jnp.where(same, line, 0.0), axis=1, keepdims=True)


def dot_0(a, b):
    return lax.dot_general(a, b, (((0,), (0,)), ((), ())), preferred_element_type=F32)


def kernel(
    cap,
    splits,
    tile,
    ids_ref,
    weight_ref,
    input_ref,
    upstream_ref,
    query_ref,
    key_ref,
    value_ref,
    gate_hbm,
    up_hbm,
    down_hbm,
    proj_hbm,
    resid_ref,
    query_grad_ref,
    key_grad_ref,
    value_grad_ref,
    slots,
    received,
    w_gate,
    w_up,
    w_down,
    part,
    rep_in,
    half,
    sub_in,
    grads,
    out,
    returned,
    proj,
    keys_ext,
    values_ext,
    probs,
    attended,
    query_dots,
    state,
    state_in,
    before,
    grad_state,
    grad_state_in,
    after,
    full,
    head_grad,
    query_sum,
    key_sum,
    value_sum,
    carry,
    carry_in,
    w_sem,
    own_sem,
    in_send,
    in_recv,
    rep_send,
    rep_recv,
    sub_send,
    sub_recv,
    agx_send,
    agx_recv,
    agr_send,
    agr_recv,
    out_send,
    out_recv,
    halo_send,
    halo_recv,
    state_send,
    state_recv,
    after_send,
    after_recv,
    resx_send,
    resx_recv,
    resr_send,
    resr_recv,
    carry_send,
    carry_recv,
):
    seqs, subs, reps = lax.axis_size("seq"), lax.axis_size("sub"), lax.axis_size("rep")
    seq, sub, rep = lax.axis_index("seq"), lax.axis_index("sub"), lax.axis_index("rep")
    local_experts, features, hidden = gate_hbm.shape
    experts = local_experts * seqs
    half_rows = half.shape[2]
    piece_rows = half_rows // subs
    block = seqs * cap
    chunks = local_experts * splits
    sent = []
    sent_if = []
    rows = ids_ref.shape[1]
    heads = features // HEAD_DIM
    window = WINDOW
    pieces = subs * reps

    def send_if(cond, src, dst, send_sem, recv_sem, device):
        copy = pltpu.make_async_remote_copy(
            src_ref=src,
            dst_ref=dst,
            send_sem=send_sem,
            recv_sem=recv_sem,
            device_id=device,
            device_id_type=MESH,
        )
        pl.when(cond)(copy.start)
        sent_if.append((cond, copy))

    def of_head(h):
        return pl.ds(h * HEAD_DIM, HEAD_DIM)

    weight_copies = [
        pltpu.make_async_copy(gate_hbm, w_gate, w_sem.at[0]),
        pltpu.make_async_copy(up_hbm, w_up, w_sem.at[1]),
        pltpu.make_async_copy(down_hbm, w_down, w_sem.at[2]),
        pltpu.make_async_copy(proj_hbm, proj, w_sem.at[3]),
    ]
    for copy in weight_copies:
        copy.start()

    def slot_rows(owner, c):
        return pl.ds(pl.multiple_of(c * block + owner * cap, 16), cap)

    def source_rows(source):
        return pl.ds(pl.multiple_of(source * cap, 16), cap)

    def half_of(r):
        return pl.ds(pl.multiple_of(r * half_rows, 16), half_rows)

    def piece_of(s):
        return pl.ds(pl.multiple_of(s * piece_rows, 16), piece_rows)

    def rows_of(r, s):
        return pl.ds(pl.multiple_of(r * half_rows + s * piece_rows, 16), piece_rows)

    places = slots_of(ids_ref[...], local_experts, splits, cap, seqs)

    def fill(c):
        slot_at = lax.broadcasted_iota(jnp.int32, (block, rows), 0).astype(F32) + float(c * block)
        pick = jnp.zeros(slot_at.shape, F32)
        for place in places:
            pick = pick + (slot_at == place).astype(F32)
        pick = pick.astype(BF16)
        slots[c * block : (c + 1) * block, :features] = dot(pick, input_ref[...]).astype(BF16)
        slots[c * block : (c + 1) * block, features:] = dot(pick, upstream_ref[...]).astype(BF16)

    own = [None] * chunks
    batches = [None] * chunks

    def start(c):
        own[c] = pltpu.make_async_copy(
            slots.at[slot_rows(seq, c)], received.at[c, source_rows(seq)], own_sem.at[c]
        )
        own[c].start()
        batches[c] = []
        for off in range(1, seqs):
            target = lax.rem(seq + off, seqs)
            batches[c].append(
                send(
                    slots.at[slot_rows(target, c)],
                    received.at[c, source_rows(seq)],
                    in_send.at[c, off - 1],
                    in_recv.at[c, off - 1],
                    {"seq": target},
                )
            )

    def left(c):
        for copy in batches[c]:
            copy.wait_send()

    def first_products(e):
        own[e].wait()
        for off in range(1, seqs):
            source = lax.rem(seq + seqs - off, seqs)
            arrived(received.at[e, source_rows(source)], in_recv.at[e, off - 1])
        for a in range(3):

            @pl.loop(0, hidden // tile)
            def _(j):
                cols = pl.ds(pl.multiple_of(j * tile, tile), tile)
                if a == 0:
                    got = dot(received[e, :, :features], w_gate[e // splits, :, cols])
                elif a == 1:
                    got = dot(received[e, :, :features], w_up[e // splits, :, cols])
                else:
                    got = dot_t(received[e, :, features:], w_down[e // splits, cols, :])
                part[e, a, :, cols] = got.astype(BF16)

            for off in range(1, reps):
                target = lax.rem(rep + off, reps)
                sent.append(
                    send(
                        part.at[e, a, half_of(target)],
                        rep_in.at[e, a, off - 1],
                        rep_send.at[e, a, off - 1],
                        rep_recv.at[e, a, off - 1],
                        {"rep": target},
                    )
                )
        for a in range(3):
            for off in range(1, reps):
                arrived(rep_in.at[e, a, off - 1], rep_recv.at[e, a, off - 1])
            total = part[e, a, half_of(rep), :].astype(F32)
            for off in range(1, reps):
                total = total + rep_in[e, a, off - 1].astype(F32)
            half[e, a] = total.astype(BF16)
            for off in range(1, subs):
                target = lax.rem(sub + off, subs)
                sent.append(
                    send(
                        half.at[e, a, piece_of(target)],
                        sub_in.at[e, a, off - 1],
                        sub_send.at[e, a, off - 1],
                        sub_recv.at[e, a, off - 1],
                        {"sub": target},
                    )
                )

    def gate(e):
        sums = []
        for a in range(3):
            for off in range(1, subs):
                arrived(sub_in.at[e, a, off - 1], sub_recv.at[e, a, off - 1])
            total = half[e, a, piece_of(sub), :].astype(F32)
            for off in range(1, subs):
                total = total + sub_in[e, a, off - 1].astype(F32)
            sums.append(total)
        gate_grad, up_grad = silu_grads(*sums)
        mine = rows_of(rep, sub)
        grads[e, mine, :hidden] = gate_grad
        grads[e, mine, hidden:] = up_grad
        for off in range(1, subs):
            target = lax.rem(sub + off, subs)
            sent.append(
                send(
                    grads.at[e, mine],
                    grads.at[e, mine],
                    agx_send.at[e, off - 1],
                    agx_recv.at[e, off - 1],
                    {"sub": target},
                )
            )
        pass_on(e, 0)

    def pass_on(e, sub_off):
        piece = rows_of(rep, lax.rem(sub + subs - sub_off, subs))
        for off in range(1, reps):
            target = lax.rem(rep + off, reps)
            sent.append(
                send(
                    grads.at[e, piece],
                    grads.at[e, piece],
                    agr_send.at[e, off - 1, sub_off],
                    agr_recv.at[e, off - 1, sub_off],
                    {"rep": target},
                )
            )

    def second_products(e):
        for sub_off in range(1, subs):
            arrived(
                grads.at[e, rows_of(rep, lax.rem(sub + subs - sub_off, subs))],
                agx_recv.at[e, sub_off - 1],
            )
            pass_on(e, sub_off)
        for off in range(1, reps):
            for sub_off in range(subs):
                piece = rows_of(
                    lax.rem(rep + reps - off, reps), lax.rem(sub + subs - sub_off, subs)
                )
                arrived(grads.at[e, piece], agr_recv.at[e, off - 1, sub_off])

        step = min(tile, features)

        @pl.loop(0, features // step)
        def _(j):
            cols = pl.ds(pl.multiple_of(j * step, step), step)
            got = dot_t(grads[e, :, :hidden], w_gate[e // splits, cols, :])
            got = got + dot_t(grads[e, :, hidden:], w_up[e // splits, cols, :])
            out[e, :, cols] = got.astype(BF16)

        copy = pltpu.make_async_copy(
            out.at[e, source_rows(seq)], returned.at[slot_rows(seq, e)], own_sem.at[e]
        )
        copy.start()
        own[e] = copy
        for off in range(1, seqs):
            target = lax.rem(seq + off, seqs)
            sent.append(
                send(
                    out.at[e, source_rows(target)],
                    returned.at[slot_rows(seq, e)],
                    out_send.at[e, off - 1],
                    out_recv.at[e, off - 1],
                    {"seq": target},
                )
            )

    def own_parts():
        keys_ext[window:, :] = key_ref[...]
        values_ext[window:, :] = value_ref[...]

        @pl.when(seq == 0)
        def _():
            keys_ext[:window, :] = jnp.zeros((window, features), BF16)
            values_ext[:window, :] = jnp.zeros((window, features), BF16)

        @pl.when(seq == seqs - 1)
        def _():
            carry_in[...] = jnp.zeros(carry_in.shape, BF16)

        causal = lax.broadcasted_iota(jnp.int32, (rows, rows), 0) >= lax.broadcasted_iota(
            jnp.int32, (rows, rows), 1
        )
        for h in range(heads):
            cols = of_head(h)
            q, k, v = query_ref[:, cols], key_ref[:, cols], value_ref[:, cols]
            state[h] = dot_0(k, v).astype(BF16)
            query_dots[h] = jnp.where(causal, dot_t(q, k), 0.0).astype(BF16)
        before[...] = jnp.zeros(before.shape, F32)
        after[...] = jnp.zeros(after.shape, F32)

    def send_halos():
        tail = pl.ds(rows - window, window)
        for n, (src, dst) in enumerate(((key_ref, keys_ext), (value_ref, values_ext))):
            send_if(
                seq < seqs - 1,
                src.at[tail],
                dst.at[pl.ds(0, window)],
                halo_send.at[n],
                halo_recv.at[n],
                {"seq": lax.rem(seq + 1, seqs)},
            )

    def send_states():
        for off in range(1, seqs):
            send_if(
                seq + off < seqs,
                state,
                state_in.at[off - 1],
                state_send.at[off - 1],
                state_recv.at[off - 1],
                {"seq": lax.rem(seq + off, seqs)},
            )

    def window_probs():
        @pl.when(seq > 0)
        def _():
            for n, dst in enumerate((keys_ext, values_ext)):
                arrived(dst.at[pl.ds(0, window)], halo_recv.at[n])

        shape = (rows, rows + window)
        query_pos = lax.broadcasted_iota(jnp.int32, shape, 0)
        key_pos = lax.broadcasted_iota(jnp.int32, shape, 1)
        allowed = (
            (key_pos > query_pos)
            & (key_pos <= query_pos + window)
            & (key_pos + (seq * rows - window) >= 0)
        )
        for h in range(heads):
            cols = of_head(h)
            scores = dot_t(query_ref[:, cols], keys_ext[:, cols]) * (HEAD_DIM**-0.5)
            scores = jnp.where(allowed, scores, -jnp.inf)
            weights = jnp.exp(scores - jnp.max(scores, axis=1, keepdims=True))
            softmax = weights / jnp.sum(weights, axis=1, keepdims=True)
            probs[h] = softmax
            attended[:, cols] = dot(softmax.astype(BF16), values_ext[:, cols])

    def states_before():
        for off in range(1, seqs):

            @pl.when(seq >= off)
            def _():
                arrived(state_in.at[off - 1], state_recv.at[off - 1])
                before[...] = before[...] + state_in[off - 1].astype(F32)

    fill(0)
    greet(("seq", "sub", "rep"))
    start(0)
    for c in range(1, chunks):
        fill(c)
    own_parts()
    columns = [as_column(place) for place in places]
    pair_weights = [as_column(weight_ref[k : k + 1, :]) for k in range(len(places))]
    left(0)
    if chunks > 1:
        start(1)
    for copy in weight_copies:
        copy.wait()
    for c in range(chunks):
        first_products(c)
        if c + 1 < chunks:
            left(c + 1)
        if c + 2 < chunks:
            start(c + 2)
        if c == chunks - 1:
            send_halos()
        if c > 0:
            second_products(c - 1)
        gate(c)
    second_products(chunks - 1)
    window_probs()

    combined = upstream_ref[...].astype(F32)
    for c in range(chunks):
        slot_at = lax.broadcasted_iota(jnp.int32, (rows, block), 1).astype(F32) + float(c * block)
        own[c].wait()
        for off in range(1, seqs):
            source = lax.rem(seq + seqs - off, seqs)
            arrived(returned.at[slot_rows(source, c)], out_recv.at[c, off - 1])
        for pair_weight, column in zip(pair_weights, columns):
            pick = (slot_at == column).astype(BF16)
            combined = combined + pair_weight * dot(
                pick, returned[c * block : (c + 1) * block, :]
            )
    resid = combined.astype(BF16)
    resid_ref[...] = resid

    def index_of(s, r):
        return s * reps + r

    def resid_on(sub_off):
        piece = index_of(lax.rem(sub + subs - sub_off, subs), rep)
        for off in range(1, reps):
            sent.append(
                send(
                    full.at[piece],
                    full.at[piece],
                    resr_send.at[off - 1, sub_off],
                    resr_recv.at[off - 1, sub_off],
                    {"rep": lax.rem(rep + off, reps)},
                )
            )

    def project(piece):
        cols = pl.ds(pl.multiple_of(piece * features, 128), features)
        return dot_t(full[piece], proj[:, cols])

    mine = index_of(sub, rep)
    full[mine] = resid
    for off in range(1, subs):
        sent.append(
            send(
                full.at[mine],
                full.at[mine],
                resx_send.at[off - 1],
                resx_recv.at[off - 1],
                {"sub": lax.rem(sub + off, subs)},
            )
        )
    resid_on(0)
    send_states()
    total = project(mine)
    for sub_off in range(subs):
        from_sub = lax.rem(sub + subs - sub_off, subs)
        if sub_off > 0:
            piece = index_of(from_sub, rep)
            arrived(full.at[piece], resx_recv.at[sub_off - 1])
            resid_on(sub_off)
            total = total + project(piece)
        for off in range(1, reps):
            piece = index_of(from_sub, lax.rem(rep + reps - off, reps))
            arrived(full.at[piece], resr_recv.at[off - 1, sub_off])
            total = total + project(piece)
    head_grad[...] = total.astype(BF16)

    for h in range(heads):
        cols = of_head(h)
        grad_state[h] = dot_0(query_ref[:, cols], head_grad[:, cols]).astype(BF16)
    for off in range(1, seqs):
        send_if(
            seq >= off,
            grad_state,
            grad_state_in.at[off - 1],
            after_send.at[off - 1],
            after_recv.at[off - 1],
            {"seq": lax.rem(seq + seqs - off, seqs)},
        )

    scaling = HEAD_DIM**-0.5
    for h in range(heads):
        cols = of_head(h)
        q, o = query_ref[:, cols], head_grad[:, cols]
        keys, values = keys_ext[:, cols], values_ext[:, cols]
        softmax = probs[h]
        centre = jnp.sum(o.astype(F32) * attended[:, cols], axis=1, keepdims=True)
        score_grad = (softmax * (dot_t(o, values) - centre)).astype(BF16)
        query_sum[:, cols] = dot(score_grad, keys) * scaling
        key_ext = dot_0(score_grad, q) * scaling
        value_ext = dot_0(softmax.astype(BF16), o)
        key_sum[:, cols] = key_ext[window:]
        value_sum[:, cols] = value_ext[window:]
        carry[0, :, cols] = key_ext[:window].astype(BF16)
        carry[1, :, cols] = value_ext[:window].astype(BF16)
    send_if(
        seq > 0,
        carry,
        carry_in,
        carry_send.at[0],
        carry_recv.at[0],
        {"seq": lax.rem(seq + seqs - 1, seqs)},
    )

    linear = float(HEAD_DIM * rows * seqs) ** -0.5
    causal = lax.broadcasted_iota(jnp.int32, (rows, rows), 0) >= lax.broadcasted_iota(
        jnp.int32, (rows, rows), 1
    )
    for h in range(heads):
        cols = of_head(h)
        q, k, v, o = query_ref[:, cols], key_ref[:, cols], value_ref[:, cols], head_grad[:, cols]
        value_dots = jnp.where(causal, dot_t(o, v), 0.0).astype(BF16)
        query_sum[:, cols] = query_sum[:, cols] + linear * dot(value_dots, k)
        key_sum[:, cols] = key_sum[:, cols] + linear * dot_0(value_dots, q)
        value_sum[:, cols] = value_sum[:, cols] + linear * dot_0(query_dots[h], o)

    states_before()
    for h in range(heads):
        cols = of_head(h)
        lin_query = dot_t(head_grad[:, cols], before[h].astype(BF16))
        query_grad_ref[:, cols] = (query_sum[:, cols] + linear * lin_query).astype(BF16)
    for off in range(1, seqs):

        @pl.when(seq + off < seqs)
        def _():
            arrived(grad_state_in.at[off - 1], after_recv.at[off - 1])
            after[...] = after[...] + grad_state_in[off - 1].astype(F32)

    @pl.when(seq < seqs - 1)
    def _():
        arrived(carry_in, carry_recv.at[0])

    for h in range(heads):
        cols = of_head(h)
        k, v = key_ref[:, cols], value_ref[:, cols]
        later = after[h].astype(BF16)
        key_total = key_sum[:, cols] + linear * dot_t(v, later)
        value_total = value_sum[:, cols] + linear * dot(k, later)
        low = rows - window
        key_grad_ref[:low, cols] = key_total[:low].astype(BF16)
        value_grad_ref[:low, cols] = value_total[:low].astype(BF16)
        key_grad_ref[low:, cols] = (key_total[low:] + carry_in[0, :, cols].astype(F32)).astype(BF16)
        value_grad_ref[low:, cols] = (
            value_total[low:] + carry_in[1, :, cols].astype(F32)
        ).astype(BF16)
    for copy in sent:
        copy.wait_send()
    for cond, copy in sent_if:
        pl.when(cond)(copy.wait_send)


def local(
    moe_input,
    upstream,
    expert_ids,
    router_weight,
    w_gate,
    w_up,
    w_down,
    out_proj,
    query,
    key_in,
    value,
):
    rows, features = moe_input.shape
    seqs, subs, reps = lax.axis_size("seq"), lax.axis_size("sub"), lax.axis_size("rep")
    local_experts, _, hidden = w_gate.shape
    experts = local_experts * seqs
    cap = max(2, 3 * rows // experts)
    cap = -(-cap // 16) * 16
    while seqs * cap % (16 * subs * reps):
        cap += 16
    splits = SPLITS
    while cap % (16 * splits) or seqs * cap // splits % (16 * subs * reps):
        splits -= 1
    slot_count = experts * cap
    cap = cap // splits
    tile = 256 if hidden % 256 == 0 else hidden
    block = seqs * cap
    half_rows = block // reps
    piece_rows = half_rows // subs
    vmem = pl.BlockSpec(memory_space=pltpu.VMEM)
    hbm = pl.BlockSpec(memory_space=pl.ANY)
    dma = pltpu.SemaphoreType.DMA
    n = local_experts * splits
    heads = features // HEAD_DIM
    states = (heads, HEAD_DIM, HEAD_DIM)
    results = pl.pallas_call(
        functools.partial(kernel, cap, splits, tile),
        out_shape=[jax.ShapeDtypeStruct((rows, features), BF16)] * 4,
        in_specs=[vmem] * 7 + [hbm] * 4,
        out_specs=[vmem] * 4,
        scratch_shapes=[
            pltpu.VMEM((slot_count, 2 * features), BF16),
            pltpu.VMEM((n, block, 2 * features), BF16),
            pltpu.VMEM(w_gate.shape, BF16),
            pltpu.VMEM(w_up.shape, BF16),
            pltpu.VMEM(w_down.shape, BF16),
            pltpu.VMEM((n, 3, block, hidden), BF16),
            pltpu.VMEM((n, 3, reps - 1, half_rows, hidden), BF16),
            pltpu.VMEM((n, 3, half_rows, hidden), BF16),
            pltpu.VMEM((n, 3, subs - 1, piece_rows, hidden), BF16),
            pltpu.VMEM((n, block, 2 * hidden), BF16),
            pltpu.VMEM((n, block, features), BF16),
            pltpu.VMEM((slot_count, features), BF16),
            pltpu.VMEM(out_proj.shape, BF16),
            pltpu.VMEM((rows + WINDOW, features), BF16),
            pltpu.VMEM((rows + WINDOW, features), BF16),
            pltpu.VMEM((heads, rows, rows + WINDOW), F32),
            pltpu.VMEM((rows, features), F32),
            pltpu.VMEM((heads, rows, rows), BF16),
            pltpu.VMEM(states, BF16),
            pltpu.VMEM((seqs - 1,) + states, BF16),
            pltpu.VMEM(states, F32),
            pltpu.VMEM(states, BF16),
            pltpu.VMEM((seqs - 1,) + states, BF16),
            pltpu.VMEM(states, F32),
            pltpu.VMEM((subs * reps, rows, features), BF16),
            pltpu.VMEM((rows, features), BF16),
            pltpu.VMEM((rows, features), F32),
            pltpu.VMEM((rows, features), F32),
            pltpu.VMEM((rows, features), F32),
            pltpu.VMEM((2, WINDOW, features), BF16),
            pltpu.VMEM((2, WINDOW, features), BF16),
            dma((4,)),
            dma((n,)),
            dma((n, seqs - 1)),
            dma((n, seqs - 1)),
            dma((n, 3, reps - 1)),
            dma((n, 3, reps - 1)),
            dma((n, 3, subs - 1)),
            dma((n, 3, subs - 1)),
            dma((n, subs - 1)),
            dma((n, subs - 1)),
            dma((n, reps - 1, subs)),
            dma((n, reps - 1, subs)),
            dma((n, seqs - 1)),
            dma((n, seqs - 1)),
            dma((2,)),
            dma((2,)),
            dma((seqs - 1,)),
            dma((seqs - 1,)),
            dma((seqs - 1,)),
            dma((seqs - 1,)),
            dma((subs - 1,)),
            dma((subs - 1,)),
            dma((reps - 1, subs)),
            dma((reps - 1, subs)),
            dma((1,)),
            dma((1,)),
        ],
        compiler_params=pltpu.CompilerParams(
            collective_id=0, has_side_effects=True, vmem_limit_bytes=56 * 1024 * 1024
        ),
        name="backward",
    )(
        expert_ids.T,
        router_weight.T,
        moe_input,
        upstream,
        query,
        key_in,
        value,
        w_gate,
        w_up,
        w_down,
        out_proj,
    )
    return pl.pallas_call(
        place_kernel,
        out_shape=[jax.ShapeDtypeStruct((rows, features), BF16)] * 4,
        in_specs=[vmem] * 4,
        out_specs=[vmem] * 4,
        name="place",
    )(*results)


def place_kernel(*refs):
    for src, dst in zip(refs[:4], refs[4:]):
        dst[...] = src[...]


def solution(mesh):
    return jax.shard_map(
        local,
        mesh=mesh,
        in_specs=(
            P(("groups", "seq"), ("sub", "rep")),
            P(("groups", "seq"), ("sub", "rep")),
            P(("groups", "seq"), None),
            P(("groups", "seq"), None),
            P("seq", ("sub", "rep"), None),
            P("seq", ("sub", "rep"), None),
            P("seq", None, ("sub", "rep")),
            P(("sub", "rep"), None),
            P(("groups", "seq"), ("sub", "rep")),
            P(("groups", "seq"), ("sub", "rep")),
            P(("groups", "seq"), ("sub", "rep")),
        ),
        out_specs=(
            P(("groups", "seq"), ("sub", "rep")),
            P(("groups", "seq"), ("sub", "rep")),
            P(("groups", "seq"), ("sub", "rep")),
            P(("groups", "seq"), ("sub", "rep")),
        ),
        check_vma=False,
    )
```

```python
import functools

import jax
import jax.numpy as jnp
from jax import lax
from jax.experimental import pallas as pl
from jax.experimental.pallas import tpu as pltpu
from jax.sharding import PartitionSpec as P

HEAD_DIM = 128
WINDOW = 128
SPLITS = 3
MESH = pl.DeviceIdType.MESH
F32 = jnp.float32
BF16 = jnp.bfloat16


def silu_grads(pre_gate, pre_up, hidden_grad):
    sigmoid_gate = jax.nn.sigmoid(pre_gate)
    gate_grad = hidden_grad * pre_up * sigmoid_gate * (1.0 + pre_gate * (1.0 - sigmoid_gate))
    up_grad = hidden_grad * pre_gate * sigmoid_gate
    return (gate_grad.astype(jnp.bfloat16), up_grad.astype(jnp.bfloat16))


def dot(a, b):
    return jnp.dot(a, b, preferred_element_type=F32)


def dot_t(a, b):
    return lax.dot_general(a, b, (((1,), (1,)), ((), ())), preferred_element_type=F32)


def arrived(ref, sem):
    pltpu.make_async_copy(ref, ref, sem).wait()


def send(src, dst, send_sem, recv_sem, device):
    copy = pltpu.make_async_remote_copy(
        src_ref=src,
        dst_ref=dst,
        send_sem=send_sem,
        recv_sem=recv_sem,
        device_id=device,
        device_id_type=MESH,
    )
    copy.start()
    return copy


def greet(axes):
    barrier = pltpu.get_barrier_semaphore()
    count = 0
    for axis in axes:
        size, me = lax.axis_size(axis), lax.axis_index(axis)
        for off in range(1, size):
            pl.semaphore_signal(
                barrier, inc=1, device_id={axis: lax.rem(me + off, size)}, device_id_type=MESH
            )
            count += 1
    pl.semaphore_wait(barrier, count)


def slots_of(ids, local_experts, splits, chunk_cap, seqs):
    chosen, rows = ids.shape
    block = seqs * chunk_cap
    experts = lax.broadcasted_iota(jnp.int32, (local_experts * seqs, rows), 0)
    named = [(experts == ids[k : k + 1, :]).astype(F32) for k in range(chosen)]
    earlier = (
        lax.broadcasted_iota(jnp.int32, (rows, rows), 0)
        < lax.broadcasted_iota(jnp.int32, (rows, rows), 1)
    ).astype(BF16)
    rank = dot(sum(named).astype(BF16), earlier)
    owner = jnp.zeros(experts.shape, F32)
    for i in range(1, seqs):
        owner = owner + (experts >= i * local_experts).astype(F32)
    local = experts.astype(F32) - owner * local_experts
    first = local * (splits * block) + owner * chunk_cap
    places = []
    for n in named:
        own_rank = jnp.sum(n * rank, axis=0, keepdims=True)
        place = jnp.sum(n * first, axis=0, keepdims=True) + own_rank
        for i in range(1, splits):
            place = place + (own_rank >= i * chunk_cap).astype(F32) * (block - chunk_cap)
        places.append(place)
    return places


def as_column(line):
    count = line.shape[1]
    same = lax.broadcasted_iota(jnp.int32, (count, count), 0) == lax.broadcasted_iota(
        jnp.int32, (count, count), 1
    )
    return jnp.sum(jnp.where(same, line, 0.0), axis=1, keepdims=True)


def dot_0(a, b):
    return lax.dot_general(a, b, (((0,), (0,)), ((), ())), preferred_element_type=F32)


def kernel(
    cap,
    splits,
    tile,
    ids_ref,
    weight_ref,
    input_ref,
    upstream_ref,
    query_ref,
    key_ref,
    value_ref,
    gate_hbm,
    up_hbm,
    down_hbm,
    proj_hbm,
    resid_ref,
    query_grad_ref,
    key_grad_ref,
    value_grad_ref,
    slots,
    received,
    w_gate,
    w_up,
    w_down,
    part,
    rep_in,
    half,
    sub_in,
    grads,
    out,
    returned,
    proj,
    keys_ext,
    values_ext,
    probs,
    attended,
    query_dots,
    state,
    state_in,
    before,
    grad_state,
    grad_state_in,
    after,
    full,
    head_grad,
    query_sum,
    key_sum,
    value_sum,
    carry,
    carry_in,
    w_sem,
    own_sem,
    in_send,
    in_recv,
    rep_send,
    rep_recv,
    sub_send,
    sub_recv,
    agx_send,
    agx_recv,
    agr_send,
    agr_recv,
    out_send,
    out_recv,
    halo_send,
    halo_recv,
    state_send,
    state_recv,
    after_send,
    after_recv,
    resx_send,
    resx_recv,
    resr_send,
    resr_recv,
    carry_send,
    carry_recv,
):
    seqs, subs, reps = lax.axis_size("seq"), lax.axis_size("sub"), lax.axis_size("rep")
    seq, sub, rep = lax.axis_index("seq"), lax.axis_index("sub"), lax.axis_index("rep")
    local_experts, features, hidden = gate_hbm.shape
    experts = local_experts * seqs
    half_rows = half.shape[2]
    piece_rows = half_rows // subs
    block = seqs * cap
    chunks = local_experts * splits
    sent = []
    sent_if = []
    rows = ids_ref.shape[1]
    heads = features // HEAD_DIM
    window = WINDOW
    pieces = subs * reps

    def send_if(cond, src, dst, send_sem, recv_sem, device):
        copy = pltpu.make_async_remote_copy(
            src_ref=src,
            dst_ref=dst,
            send_sem=send_sem,
            recv_sem=recv_sem,
            device_id=device,
            device_id_type=MESH,
        )
        pl.when(cond)(copy.start)
        sent_if.append((cond, copy))

    def of_head(h):
        return pl.ds(h * HEAD_DIM, HEAD_DIM)

    weight_copies = [
        pltpu.make_async_copy(gate_hbm, w_gate, w_sem.at[0]),
        pltpu.make_async_copy(up_hbm, w_up, w_sem.at[1]),
        pltpu.make_async_copy(down_hbm, w_down, w_sem.at[2]),
        pltpu.make_async_copy(proj_hbm, proj, w_sem.at[3]),
    ]
    for copy in weight_copies:
        copy.start()

    def slot_rows(owner, c):
        return pl.ds(pl.multiple_of(c * block + owner * cap, 16), cap)

    def source_rows(source):
        return pl.ds(pl.multiple_of(source * cap, 16), cap)

    def half_of(r):
        return pl.ds(pl.multiple_of(r * half_rows, 16), half_rows)

    def piece_of(s):
        return pl.ds(pl.multiple_of(s * piece_rows, 16), piece_rows)

    def rows_of(r, s):
        return pl.ds(pl.multiple_of(r * half_rows + s * piece_rows, 16), piece_rows)

    places = slots_of(ids_ref[...], local_experts, splits, cap, seqs)

    def fill(c):
        slot_at = lax.broadcasted_iota(jnp.int32, (block, rows), 0).astype(F32) + float(c * block)
        pick = jnp.zeros(slot_at.shape, F32)
        for place in places:
            pick = pick + (slot_at == place).astype(F32)
        pick = pick.astype(BF16)
        slots[c * block : (c + 1) * block, :features] = dot(pick, input_ref[...]).astype(BF16)
        slots[c * block : (c + 1) * block, features:] = dot(pick, upstream_ref[...]).astype(BF16)

    own = [None] * chunks
    batches = [None] * chunks

    def start(c):
        own[c] = pltpu.make_async_copy(
            slots.at[slot_rows(seq, c)], received.at[c, source_rows(seq)], own_sem.at[c]
        )
        own[c].start()
        batches[c] = []
        for off in range(1, seqs):
            target = lax.rem(seq + off, seqs)
            batches[c].append(
                send(
                    slots.at[slot_rows(target, c)],
                    received.at[c, source_rows(seq)],
                    in_send.at[c, off - 1],
                    in_recv.at[c, off - 1],
                    {"seq": target},
                )
            )

    def left(c):
        for copy in batches[c]:
            copy.wait_send()

    def first_products(e):
        own[e].wait()
        for off in range(1, seqs):
            source = lax.rem(seq + seqs - off, seqs)
            arrived(received.at[e, source_rows(source)], in_recv.at[e, off - 1])
        if e + 2 < chunks:
            start(e + 2)
        for a in range(3):

            @pl.loop(0, hidden // tile)
            def _(j):
                cols = pl.ds(pl.multiple_of(j * tile, tile), tile)
                if a == 0:
                    got = dot(received[e, :, :features], w_gate[e // splits, :, cols])
                elif a == 1:
                    got = dot(received[e, :, :features], w_up[e // splits, :, cols])
                else:
                    got = dot_t(received[e, :, features:], w_down[e // splits, cols, :])
                part[e, a, :, cols] = got.astype(BF16)

            for off in range(1, reps):
                target = lax.rem(rep + off, reps)
                sent.append(
                    send(
                        part.at[e, a, half_of(target)],
                        rep_in.at[e, a, off - 1],
                        rep_send.at[e, a, off - 1],
                        rep_recv.at[e, a, off - 1],
                        {"rep": target},
                    )
                )

    def chip_sums(e):
        for a in range(3):
            for off in range(1, reps):
                arrived(rep_in.at[e, a, off - 1], rep_recv.at[e, a, off - 1])
            total = part[e, a, half_of(rep), :].astype(F32)
            for off in range(1, reps):
                total = total + rep_in[e, a, off - 1].astype(F32)
            half[e, a] = total.astype(BF16)
            for off in range(1, subs):
                target = lax.rem(sub + off, subs)
                sent.append(
                    send(
                        half.at[e, a, piece_of(target)],
                        sub_in.at[e, a, off - 1],
                        sub_send.at[e, a, off - 1],
                        sub_recv.at[e, a, off - 1],
                        {"sub": target},
                    )
                )

    def gate(e):
        sums = []
        for a in range(3):
            for off in range(1, subs):
                arrived(sub_in.at[e, a, off - 1], sub_recv.at[e, a, off - 1])
            total = half[e, a, piece_of(sub), :].astype(F32)
            for off in range(1, subs):
                total = total + sub_in[e, a, off - 1].astype(F32)
            sums.append(total)
        gate_grad, up_grad = silu_grads(*sums)
        mine = rows_of(rep, sub)
        grads[e, mine, :hidden] = gate_grad
        grads[e, mine, hidden:] = up_grad
        for off in range(1, subs):
            target = lax.rem(sub + off, subs)
            sent.append(
                send(
                    grads.at[e, mine],
                    grads.at[e, mine],
                    agx_send.at[e, off - 1],
                    agx_recv.at[e, off - 1],
                    {"sub": target},
                )
            )
        pass_on(e, 0)

    def pass_on(e, sub_off):
        piece = rows_of(rep, lax.rem(sub + subs - sub_off, subs))
        for off in range(1, reps):
            target = lax.rem(rep + off, reps)
            sent.append(
                send(
                    grads.at[e, piece],
                    grads.at[e, piece],
                    agr_send.at[e, off - 1, sub_off],
                    agr_recv.at[e, off - 1, sub_off],
                    {"rep": target},
                )
            )

    def forward(e):
        for sub_off in range(1, subs):
            arrived(
                grads.at[e, rows_of(rep, lax.rem(sub + subs - sub_off, subs))],
                agx_recv.at[e, sub_off - 1],
            )
            pass_on(e, sub_off)

    def second_products(e):
        for off in range(1, reps):
            for sub_off in range(subs):
                piece = rows_of(
                    lax.rem(rep + reps - off, reps), lax.rem(sub + subs - sub_off, subs)
                )
                arrived(grads.at[e, piece], agr_recv.at[e, off - 1, sub_off])

        step = min(tile, features)

        @pl.loop(0, features // step)
        def _(j):
            cols = pl.ds(pl.multiple_of(j * step, step), step)
            got = dot_t(grads[e, :, :hidden], w_gate[e // splits, cols, :])
            got = got + dot_t(grads[e, :, hidden:], w_up[e // splits, cols, :])
            out[e, :, cols] = got.astype(BF16)

        copy = pltpu.make_async_copy(
            out.at[e, source_rows(seq)], returned.at[slot_rows(seq, e)], own_sem.at[e]
        )
        copy.start()
        own[e] = copy
        for off in range(1, seqs):
            target = lax.rem(seq + off, seqs)
            sent.append(
                send(
                    out.at[e, source_rows(target)],
                    returned.at[slot_rows(seq, e)],
                    out_send.at[e, off - 1],
                    out_recv.at[e, off - 1],
                    {"seq": target},
                )
            )

    def own_parts():
        keys_ext[window:, :] = key_ref[...]
        values_ext[window:, :] = value_ref[...]

        @pl.when(seq == 0)
        def _():
            keys_ext[:window, :] = jnp.zeros((window, features), BF16)
            values_ext[:window, :] = jnp.zeros((window, features), BF16)

        @pl.when(seq == seqs - 1)
        def _():
            carry_in[...] = jnp.zeros(carry_in.shape, BF16)

        causal = lax.broadcasted_iota(jnp.int32, (rows, rows), 0) >= lax.broadcasted_iota(
            jnp.int32, (rows, rows), 1
        )
        for h in range(heads):
            cols = of_head(h)
            q, k, v = query_ref[:, cols], key_ref[:, cols], value_ref[:, cols]
            state[h] = dot_0(k, v).astype(BF16)
            query_dots[h] = jnp.where(causal, dot_t(q, k), 0.0).astype(BF16)
        before[...] = jnp.zeros(before.shape, F32)
        after[...] = jnp.zeros(after.shape, F32)

    def send_halos():
        tail = pl.ds(rows - window, window)
        for n, (src, dst) in enumerate(((key_ref, keys_ext), (value_ref, values_ext))):
            send_if(
                seq < seqs - 1,
                src.at[tail],
                dst.at[pl.ds(0, window)],
                halo_send.at[n],
                halo_recv.at[n],
                {"seq": lax.rem(seq + 1, seqs)},
            )

    def send_states():
        for off in range(1, seqs):
            send_if(
                seq + off < seqs,
                state,
                state_in.at[off - 1],
                state_send.at[off - 1],
                state_recv.at[off - 1],
                {"seq": lax.rem(seq + off, seqs)},
            )

    def window_probs():
        @pl.when(seq > 0)
        def _():
            for n, dst in enumerate((keys_ext, values_ext)):
                arrived(dst.at[pl.ds(0, window)], halo_recv.at[n])

        shape = (rows, rows + window)
        query_pos = lax.broadcasted_iota(jnp.int32, shape, 0)
        key_pos = lax.broadcasted_iota(jnp.int32, shape, 1)
        allowed = (
            (key_pos > query_pos)
            & (key_pos <= query_pos + window)
            & (key_pos + (seq * rows - window) >= 0)
        )
        for h in range(heads):
            cols = of_head(h)
            scores = dot_t(query_ref[:, cols], keys_ext[:, cols]) * (HEAD_DIM**-0.5)
            scores = jnp.where(allowed, scores, -jnp.inf)
            weights = jnp.exp(scores - jnp.max(scores, axis=1, keepdims=True))
            softmax = weights / jnp.sum(weights, axis=1, keepdims=True)
            probs[h] = softmax
            attended[:, cols] = dot(softmax.astype(BF16), values_ext[:, cols])

    def states_before():
        for off in range(1, seqs):

            @pl.when(seq >= off)
            def _():
                arrived(state_in.at[off - 1], state_recv.at[off - 1])
                before[...] = before[...] + state_in[off - 1].astype(F32)

    fill(0)
    greet(("seq", "sub", "rep"))
    start(0)
    for c in range(1, chunks):
        fill(c)
    own_parts()
    columns = [as_column(place) for place in places]
    pair_weights = [as_column(weight_ref[k : k + 1, :]) for k in range(len(places))]
    left(0)
    if chunks > 1:
        start(1)
    for copy in weight_copies:
        copy.wait()
    for c in range(chunks + 2):
        if 2 <= c:
            forward(c - 2)
        if c < chunks:
            first_products(c)
        if c == chunks - 1:
            send_halos()
        if 1 <= c <= chunks:
            gate(c - 1)
        if c < chunks:
            chip_sums(c)
        if 2 <= c:
            second_products(c - 2)
    for batch in batches[1:]:
        sent.extend(batch)
    window_probs()

    combined = upstream_ref[...].astype(F32)
    for c in range(chunks):
        slot_at = lax.broadcasted_iota(jnp.int32, (rows, block), 1).astype(F32) + float(c * block)
        own[c].wait()
        for off in range(1, seqs):
            source = lax.rem(seq + seqs - off, seqs)
            arrived(returned.at[slot_rows(source, c)], out_recv.at[c, off - 1])
        for pair_weight, column in zip(pair_weights, columns):
            pick = (slot_at == column).astype(BF16)
            combined = combined + pair_weight * dot(
                pick, returned[c * block : (c + 1) * block, :]
            )
    resid = combined.astype(BF16)
    resid_ref[...] = resid

    def index_of(s, r):
        return s * reps + r

    def resid_on(sub_off):
        piece = index_of(lax.rem(sub + subs - sub_off, subs), rep)
        for off in range(1, reps):
            sent.append(
                send(
                    full.at[piece],
                    full.at[piece],
                    resr_send.at[off - 1, sub_off],
                    resr_recv.at[off - 1, sub_off],
                    {"rep": lax.rem(rep + off, reps)},
                )
            )

    def project(piece):
        cols = pl.ds(pl.multiple_of(piece * features, 128), features)
        return dot_t(full[piece], proj[:, cols])

    mine = index_of(sub, rep)
    full[mine] = resid
    for off in range(1, subs):
        sent.append(
            send(
                full.at[mine],
                full.at[mine],
                resx_send.at[off - 1],
                resx_recv.at[off - 1],
                {"sub": lax.rem(sub + off, subs)},
            )
        )
    resid_on(0)
    send_states()
    total = project(mine)
    for sub_off in range(subs):
        from_sub = lax.rem(sub + subs - sub_off, subs)
        if sub_off > 0:
            piece = index_of(from_sub, rep)
            arrived(full.at[piece], resx_recv.at[sub_off - 1])
            resid_on(sub_off)
            total = total + project(piece)
        for off in range(1, reps):
            piece = index_of(from_sub, lax.rem(rep + reps - off, reps))
            arrived(full.at[piece], resr_recv.at[off - 1, sub_off])
            total = total + project(piece)
    head_grad[...] = total.astype(BF16)

    for h in range(heads):
        cols = of_head(h)
        grad_state[h] = dot_0(query_ref[:, cols], head_grad[:, cols]).astype(BF16)
    for off in range(1, seqs):
        send_if(
            seq >= off,
            grad_state,
            grad_state_in.at[off - 1],
            after_send.at[off - 1],
            after_recv.at[off - 1],
            {"seq": lax.rem(seq + seqs - off, seqs)},
        )

    scaling = HEAD_DIM**-0.5
    for h in range(heads):
        cols = of_head(h)
        q, o = query_ref[:, cols], head_grad[:, cols]
        keys, values = keys_ext[:, cols], values_ext[:, cols]
        softmax = probs[h]
        centre = jnp.sum(o.astype(F32) * attended[:, cols], axis=1, keepdims=True)
        score_grad = (softmax * (dot_t(o, values) - centre)).astype(BF16)
        query_sum[:, cols] = dot(score_grad, keys) * scaling
        key_ext = dot_0(score_grad, q) * scaling
        value_ext = dot_0(softmax.astype(BF16), o)
        key_sum[:, cols] = key_ext[window:]
        value_sum[:, cols] = value_ext[window:]
        carry[0, :, cols] = key_ext[:window].astype(BF16)
        carry[1, :, cols] = value_ext[:window].astype(BF16)
    send_if(
        seq > 0,
        carry,
        carry_in,
        carry_send.at[0],
        carry_recv.at[0],
        {"seq": lax.rem(seq + seqs - 1, seqs)},
    )

    linear = float(HEAD_DIM * rows * seqs) ** -0.5
    causal = lax.broadcasted_iota(jnp.int32, (rows, rows), 0) >= lax.broadcasted_iota(
        jnp.int32, (rows, rows), 1
    )
    for h in range(heads):
        cols = of_head(h)
        q, k, v, o = query_ref[:, cols], key_ref[:, cols], value_ref[:, cols], head_grad[:, cols]
        value_dots = jnp.where(causal, dot_t(o, v), 0.0).astype(BF16)
        query_sum[:, cols] = query_sum[:, cols] + linear * dot(value_dots, k)
        key_sum[:, cols] = key_sum[:, cols] + linear * dot_0(value_dots, q)
        value_sum[:, cols] = value_sum[:, cols] + linear * dot_0(query_dots[h], o)

    states_before()
    for h in range(heads):
        cols = of_head(h)
        lin_query = dot_t(head_grad[:, cols], before[h].astype(BF16))
        query_grad_ref[:, cols] = (query_sum[:, cols] + linear * lin_query).astype(BF16)
    for off in range(1, seqs):

        @pl.when(seq + off < seqs)
        def _():
            arrived(grad_state_in.at[off - 1], after_recv.at[off - 1])
            after[...] = after[...] + grad_state_in[off - 1].astype(F32)

    @pl.when(seq < seqs - 1)
    def _():
        arrived(carry_in, carry_recv.at[0])

    for h in range(heads):
        cols = of_head(h)
        k, v = key_ref[:, cols], value_ref[:, cols]
        later = after[h].astype(BF16)
        key_total = key_sum[:, cols] + linear * dot_t(v, later)
        value_total = value_sum[:, cols] + linear * dot(k, later)
        low = rows - window
        key_grad_ref[:low, cols] = key_total[:low].astype(BF16)
        value_grad_ref[:low, cols] = value_total[:low].astype(BF16)
        key_grad_ref[low:, cols] = (key_total[low:] + carry_in[0, :, cols].astype(F32)).astype(BF16)
        value_grad_ref[low:, cols] = (
            value_total[low:] + carry_in[1, :, cols].astype(F32)
        ).astype(BF16)
    for copy in sent:
        copy.wait_send()
    for cond, copy in sent_if:
        pl.when(cond)(copy.wait_send)


def local(
    moe_input,
    upstream,
    expert_ids,
    router_weight,
    w_gate,
    w_up,
    w_down,
    out_proj,
    query,
    key_in,
    value,
):
    rows, features = moe_input.shape
    seqs, subs, reps = lax.axis_size("seq"), lax.axis_size("sub"), lax.axis_size("rep")
    local_experts, _, hidden = w_gate.shape
    experts = local_experts * seqs
    cap = max(2, 3 * rows // experts)
    cap = -(-cap // 16) * 16
    while seqs * cap % (16 * subs * reps):
        cap += 16
    splits = SPLITS
    while cap % (16 * splits) or seqs * cap // splits % (16 * subs * reps):
        splits -= 1
    slot_count = experts * cap
    cap = cap // splits
    tile = 256 if hidden % 256 == 0 else hidden
    block = seqs * cap
    half_rows = block // reps
    piece_rows = half_rows // subs
    vmem = pl.BlockSpec(memory_space=pltpu.VMEM)
    hbm = pl.BlockSpec(memory_space=pl.ANY)
    dma = pltpu.SemaphoreType.DMA
    n = local_experts * splits
    heads = features // HEAD_DIM
    states = (heads, HEAD_DIM, HEAD_DIM)
    results = pl.pallas_call(
        functools.partial(kernel, cap, splits, tile),
        out_shape=[jax.ShapeDtypeStruct((rows, features), BF16)] * 4,
        in_specs=[vmem] * 7 + [hbm] * 4,
        out_specs=[vmem] * 4,
        scratch_shapes=[
            pltpu.VMEM((slot_count, 2 * features), BF16),
            pltpu.VMEM((n, block, 2 * features), BF16),
            pltpu.VMEM(w_gate.shape, BF16),
            pltpu.VMEM(w_up.shape, BF16),
            pltpu.VMEM(w_down.shape, BF16),
            pltpu.VMEM((n, 3, block, hidden), BF16),
            pltpu.VMEM((n, 3, reps - 1, half_rows, hidden), BF16),
            pltpu.VMEM((n, 3, half_rows, hidden), BF16),
            pltpu.VMEM((n, 3, subs - 1, piece_rows, hidden), BF16),
            pltpu.VMEM((n, block, 2 * hidden), BF16),
            pltpu.VMEM((n, block, features), BF16),
            pltpu.VMEM((slot_count, features), BF16),
            pltpu.VMEM(out_proj.shape, BF16),
            pltpu.VMEM((rows + WINDOW, features), BF16),
            pltpu.VMEM((rows + WINDOW, features), BF16),
            pltpu.VMEM((heads, rows, rows + WINDOW), F32),
            pltpu.VMEM((rows, features), F32),
            pltpu.VMEM((heads, rows, rows), BF16),
            pltpu.VMEM(states, BF16),
            pltpu.VMEM((seqs - 1,) + states, BF16),
            pltpu.VMEM(states, F32),
            pltpu.VMEM(states, BF16),
            pltpu.VMEM((seqs - 1,) + states, BF16),
            pltpu.VMEM(states, F32),
            pltpu.VMEM((subs * reps, rows, features), BF16),
            pltpu.VMEM((rows, features), BF16),
            pltpu.VMEM((rows, features), F32),
            pltpu.VMEM((rows, features), F32),
            pltpu.VMEM((rows, features), F32),
            pltpu.VMEM((2, WINDOW, features), BF16),
            pltpu.VMEM((2, WINDOW, features), BF16),
            dma((4,)),
            dma((n,)),
            dma((n, seqs - 1)),
            dma((n, seqs - 1)),
            dma((n, 3, reps - 1)),
            dma((n, 3, reps - 1)),
            dma((n, 3, subs - 1)),
            dma((n, 3, subs - 1)),
            dma((n, subs - 1)),
            dma((n, subs - 1)),
            dma((n, reps - 1, subs)),
            dma((n, reps - 1, subs)),
            dma((n, seqs - 1)),
            dma((n, seqs - 1)),
            dma((2,)),
            dma((2,)),
            dma((seqs - 1,)),
            dma((seqs - 1,)),
            dma((seqs - 1,)),
            dma((seqs - 1,)),
            dma((subs - 1,)),
            dma((subs - 1,)),
            dma((reps - 1, subs)),
            dma((reps - 1, subs)),
            dma((1,)),
            dma((1,)),
        ],
        compiler_params=pltpu.CompilerParams(
            collective_id=0, has_side_effects=True, vmem_limit_bytes=56 * 1024 * 1024
        ),
        name="backward",
    )(
        expert_ids.T,
        router_weight.T,
        moe_input,
        upstream,
        query,
        key_in,
        value,
        w_gate,
        w_up,
        w_down,
        out_proj,
    )
    return pl.pallas_call(
        place_kernel,
        out_shape=[jax.ShapeDtypeStruct((rows, features), BF16)] * 4,
        in_specs=[vmem] * 4,
        out_specs=[vmem] * 4,
        name="place",
    )(*results)


def place_kernel(*refs):
    for src, dst in zip(refs[:4], refs[4:]):
        dst[...] = src[...]


def solution(mesh):
    return jax.shard_map(
        local,
        mesh=mesh,
        in_specs=(
            P(("groups", "seq"), ("sub", "rep")),
            P(("groups", "seq"), ("sub", "rep")),
            P(("groups", "seq"), None),
            P(("groups", "seq"), None),
            P("seq", ("sub", "rep"), None),
            P("seq", ("sub", "rep"), None),
            P("seq", None, ("sub", "rep")),
            P(("sub", "rep"), None),
            P(("groups", "seq"), ("sub", "rep")),
            P(("groups", "seq"), ("sub", "rep")),
            P(("groups", "seq"), ("sub", "rep")),
        ),
        out_specs=(
            P(("groups", "seq"), ("sub", "rep")),
            P(("groups", "seq"), ("sub", "rep")),
            P(("groups", "seq"), ("sub", "rep")),
            P(("groups", "seq"), ("sub", "rep")),
        ),
        check_vma=False,
    )
```

```python
import functools

import jax
import jax.numpy as jnp
from jax import lax
from jax.experimental import pallas as pl
from jax.experimental.pallas import tpu as pltpu
from jax.sharding import PartitionSpec as P

HEAD_DIM = 128
WINDOW = 128
SPLITS = 3
MESH = pl.DeviceIdType.MESH
F32 = jnp.float32
BF16 = jnp.bfloat16


def silu_grads(pre_gate, pre_up, hidden_grad):
    sigmoid_gate = jax.nn.sigmoid(pre_gate)
    gate_grad = hidden_grad * pre_up * sigmoid_gate * (1.0 + pre_gate * (1.0 - sigmoid_gate))
    up_grad = hidden_grad * pre_gate * sigmoid_gate
    return (gate_grad.astype(jnp.bfloat16), up_grad.astype(jnp.bfloat16))


def dot(a, b):
    return jnp.dot(a, b, preferred_element_type=F32)


def dot_t(a, b):
    return lax.dot_general(a, b, (((1,), (1,)), ((), ())), preferred_element_type=F32)


def arrived(ref, sem):
    pltpu.make_async_copy(ref, ref, sem).wait()


def send(src, dst, send_sem, recv_sem, device):
    copy = pltpu.make_async_remote_copy(
        src_ref=src,
        dst_ref=dst,
        send_sem=send_sem,
        recv_sem=recv_sem,
        device_id=device,
        device_id_type=MESH,
    )
    copy.start()
    return copy


def greet(axes):
    barrier = pltpu.get_barrier_semaphore()
    count = 0
    for axis in axes:
        size, me = lax.axis_size(axis), lax.axis_index(axis)
        for off in range(1, size):
            pl.semaphore_signal(
                barrier, inc=1, device_id={axis: lax.rem(me + off, size)}, device_id_type=MESH
            )
            count += 1
    pl.semaphore_wait(barrier, count)


def slots_of(ids, local_experts, splits, chunk_cap, seqs):
    chosen, rows = ids.shape
    block = seqs * chunk_cap
    experts = lax.broadcasted_iota(jnp.int32, (local_experts * seqs, rows), 0)
    named = [(experts == ids[k : k + 1, :]).astype(F32) for k in range(chosen)]
    earlier = (
        lax.broadcasted_iota(jnp.int32, (rows, rows), 0)
        < lax.broadcasted_iota(jnp.int32, (rows, rows), 1)
    ).astype(BF16)
    rank = dot(sum(named).astype(BF16), earlier)
    owner = jnp.zeros(experts.shape, F32)
    for i in range(1, seqs):
        owner = owner + (experts >= i * local_experts).astype(F32)
    local = experts.astype(F32) - owner * local_experts
    first = local * (splits * block) + owner * chunk_cap
    places = []
    for n in named:
        own_rank = jnp.sum(n * rank, axis=0, keepdims=True)
        place = jnp.sum(n * first, axis=0, keepdims=True) + own_rank
        for i in range(1, splits):
            place = place + (own_rank >= i * chunk_cap).astype(F32) * (block - chunk_cap)
        places.append(place)
    return places


def as_column(line):
    count = line.shape[1]
    same = lax.broadcasted_iota(jnp.int32, (count, count), 0) == lax.broadcasted_iota(
        jnp.int32, (count, count), 1
    )
    return jnp.sum(jnp.where(same, line, 0.0), axis=1, keepdims=True)


def dot_0(a, b):
    return lax.dot_general(a, b, (((0,), (0,)), ((), ())), preferred_element_type=F32)


def kernel(
    cap,
    splits,
    tile,
    ids_ref,
    weight_ref,
    input_ref,
    upstream_ref,
    query_ref,
    key_ref,
    value_ref,
    gate_hbm,
    up_hbm,
    down_hbm,
    proj_hbm,
    resid_ref,
    query_grad_ref,
    key_grad_ref,
    value_grad_ref,
    slots,
    received,
    w_gate,
    w_up,
    w_down,
    part,
    rep_in,
    half,
    sub_in,
    grads,
    out,
    returned,
    proj,
    keys_ext,
    values_ext,
    probs,
    attended,
    query_dots,
    state,
    state_in,
    before,
    grad_state,
    grad_state_in,
    after,
    full,
    head_grad,
    query_sum,
    key_sum,
    value_sum,
    carry,
    carry_in,
    w_sem,
    own_sem,
    in_send,
    in_recv,
    rep_send,
    rep_recv,
    sub_send,
    sub_recv,
    agx_send,
    agx_recv,
    agr_send,
    agr_recv,
    out_send,
    out_recv,
    halo_send,
    halo_recv,
    state_send,
    state_recv,
    after_send,
    after_recv,
    resx_send,
    resx_recv,
    resr_send,
    resr_recv,
    carry_send,
    carry_recv,
):
    seqs, subs, reps = lax.axis_size("seq"), lax.axis_size("sub"), lax.axis_size("rep")
    seq, sub, rep = lax.axis_index("seq"), lax.axis_index("sub"), lax.axis_index("rep")
    local_experts, features, hidden = gate_hbm.shape
    experts = local_experts * seqs
    half_rows = half.shape[2]
    piece_rows = half_rows // subs
    block = seqs * cap
    chunks = local_experts * splits
    sent = []
    sent_if = []
    rows = ids_ref.shape[1]
    heads = features // HEAD_DIM
    window = WINDOW
    pieces = subs * reps

    def send_if(cond, src, dst, send_sem, recv_sem, device):
        copy = pltpu.make_async_remote_copy(
            src_ref=src,
            dst_ref=dst,
            send_sem=send_sem,
            recv_sem=recv_sem,
            device_id=device,
            device_id_type=MESH,
        )
        pl.when(cond)(copy.start)
        sent_if.append((cond, copy))

    def of_head(h):
        return pl.ds(h * HEAD_DIM, HEAD_DIM)

    weight_copies = [
        pltpu.make_async_copy(gate_hbm, w_gate, w_sem.at[0]),
        pltpu.make_async_copy(up_hbm, w_up, w_sem.at[1]),
        pltpu.make_async_copy(down_hbm, w_down, w_sem.at[2]),
        pltpu.make_async_copy(proj_hbm, proj, w_sem.at[3]),
    ]
    for copy in weight_copies:
        copy.start()

    def slot_rows(owner, c):
        return pl.ds(pl.multiple_of(c * block + owner * cap, 16), cap)

    def source_rows(source):
        return pl.ds(pl.multiple_of(source * cap, 16), cap)

    def half_of(r):
        return pl.ds(pl.multiple_of(r * half_rows, 16), half_rows)

    def piece_of(s):
        return pl.ds(pl.multiple_of(s * piece_rows, 16), piece_rows)

    def rows_of(r, s):
        return pl.ds(pl.multiple_of(r * half_rows + s * piece_rows, 16), piece_rows)

    places = slots_of(ids_ref[...], local_experts, splits, cap, seqs)

    def fill(c):
        slot_at = lax.broadcasted_iota(jnp.int32, (block, rows), 0).astype(F32) + float(c * block)
        pick = jnp.zeros(slot_at.shape, F32)
        for place in places:
            pick = pick + (slot_at == place).astype(F32)
        pick = pick.astype(BF16)
        slots[c * block : (c + 1) * block, :features] = dot(pick, input_ref[...]).astype(BF16)
        slots[c * block : (c + 1) * block, features:] = dot(pick, upstream_ref[...]).astype(BF16)

    own = [None] * chunks
    batches = [None] * chunks

    def start(c):
        own[c] = pltpu.make_async_copy(
            slots.at[slot_rows(seq, c)], received.at[c, source_rows(seq)], own_sem.at[c]
        )
        own[c].start()
        batches[c] = []
        for off in range(1, seqs):
            target = lax.rem(seq + off, seqs)
            batches[c].append(
                send(
                    slots.at[slot_rows(target, c)],
                    received.at[c, source_rows(seq)],
                    in_send.at[c, off - 1],
                    in_recv.at[c, off - 1],
                    {"seq": target},
                )
            )

    def left(c):
        for copy in batches[c]:
            copy.wait_send()

    def first_products(e):
        own[e].wait()
        for off in range(1, seqs):
            source = lax.rem(seq + seqs - off, seqs)
            arrived(received.at[e, source_rows(source)], in_recv.at[e, off - 1])
        if e + 2 < chunks:
            start(e + 2)
        for a in range(3):

            @pl.loop(0, hidden // tile)
            def _(j):
                cols = pl.ds(pl.multiple_of(j * tile, tile), tile)
                if a == 0:
                    got = dot(received[e, :, :features], w_gate[e // splits, :, cols])
                elif a == 1:
                    got = dot(received[e, :, :features], w_up[e // splits, :, cols])
                else:
                    got = dot_t(received[e, :, features:], w_down[e // splits, cols, :])
                part[e, a, :, cols] = got.astype(BF16)

            for off in range(1, reps):
                target = lax.rem(rep + off, reps)
                sent.append(
                    send(
                        part.at[e, a, half_of(target)],
                        rep_in.at[e, a, off - 1],
                        rep_send.at[e, a, off - 1],
                        rep_recv.at[e, a, off - 1],
                        {"rep": target},
                    )
                )

    def chip_sums(e):
        for a in range(3):
            for off in range(1, reps):
                arrived(rep_in.at[e, a, off - 1], rep_recv.at[e, a, off - 1])
            total = part[e, a, half_of(rep), :].astype(F32)
            for off in range(1, reps):
                total = total + rep_in[e, a, off - 1].astype(F32)
            half[e, a] = total.astype(BF16)
            for off in range(1, subs):
                target = lax.rem(sub + off, subs)
                sent.append(
                    send(
                        half.at[e, a, piece_of(target)],
                        sub_in.at[e, a, off - 1],
                        sub_send.at[e, a, off - 1],
                        sub_recv.at[e, a, off - 1],
                        {"sub": target},
                    )
                )

    def gate(e):
        sums = []
        for a in range(3):
            for off in range(1, subs):
                arrived(sub_in.at[e, a, off - 1], sub_recv.at[e, a, off - 1])
            total = half[e, a, piece_of(sub), :].astype(F32)
            for off in range(1, subs):
                total = total + sub_in[e, a, off - 1].astype(F32)
            sums.append(total)
        gate_grad, up_grad = silu_grads(*sums)
        mine = rows_of(rep, sub)
        grads[e, mine, :hidden] = gate_grad
        grads[e, mine, hidden:] = up_grad
        for off in range(1, subs):
            target = lax.rem(sub + off, subs)
            sent.append(
                send(
                    grads.at[e, mine],
                    grads.at[e, mine],
                    agx_send.at[e, off - 1],
                    agx_recv.at[e, off - 1],
                    {"sub": target},
                )
            )
        pass_on(e, 0)

    def pass_on(e, sub_off):
        piece = rows_of(rep, lax.rem(sub + subs - sub_off, subs))
        for off in range(1, reps):
            target = lax.rem(rep + off, reps)
            sent.append(
                send(
                    grads.at[e, piece],
                    grads.at[e, piece],
                    agr_send.at[e, off - 1, sub_off],
                    agr_recv.at[e, off - 1, sub_off],
                    {"rep": target},
                )
            )

    def forward(e):
        for sub_off in range(1, subs):
            arrived(
                grads.at[e, rows_of(rep, lax.rem(sub + subs - sub_off, subs))],
                agx_recv.at[e, sub_off - 1],
            )
            pass_on(e, sub_off)

    def second_products(e):
        for off in range(1, reps):
            for sub_off in range(subs):
                piece = rows_of(
                    lax.rem(rep + reps - off, reps), lax.rem(sub + subs - sub_off, subs)
                )
                arrived(grads.at[e, piece], agr_recv.at[e, off - 1, sub_off])

        step = min(tile, features)

        @pl.loop(0, features // step)
        def _(j):
            cols = pl.ds(pl.multiple_of(j * step, step), step)
            got = dot_t(grads[e, :, :hidden], w_gate[e // splits, cols, :])
            got = got + dot_t(grads[e, :, hidden:], w_up[e // splits, cols, :])
            out[e, :, cols] = got.astype(BF16)

        copy = pltpu.make_async_copy(
            out.at[e, source_rows(seq)], returned.at[slot_rows(seq, e)], own_sem.at[e]
        )
        copy.start()
        own[e] = copy
        for off in range(1, seqs):
            target = lax.rem(seq + off, seqs)
            sent.append(
                send(
                    out.at[e, source_rows(target)],
                    returned.at[slot_rows(seq, e)],
                    out_send.at[e, off - 1],
                    out_recv.at[e, off - 1],
                    {"seq": target},
                )
            )

    def own_parts():
        keys_ext[window:, :] = key_ref[...]
        values_ext[window:, :] = value_ref[...]

        @pl.when(seq == 0)
        def _():
            keys_ext[:window, :] = jnp.zeros((window, features), BF16)
            values_ext[:window, :] = jnp.zeros((window, features), BF16)

        @pl.when(seq == seqs - 1)
        def _():
            carry_in[...] = jnp.zeros(carry_in.shape, BF16)

        causal = lax.broadcasted_iota(jnp.int32, (rows, rows), 0) >= lax.broadcasted_iota(
            jnp.int32, (rows, rows), 1
        )
        for h in range(heads):
            cols = of_head(h)
            q, k, v = query_ref[:, cols], key_ref[:, cols], value_ref[:, cols]
            state[h] = dot_0(k, v).astype(BF16)
            query_dots[h] = jnp.where(causal, dot_t(q, k), 0.0).astype(BF16)
        before[...] = jnp.zeros(before.shape, F32)
        after[...] = jnp.zeros(after.shape, F32)

    def send_halos():
        tail = pl.ds(rows - window, window)
        for n, (src, dst) in enumerate(((key_ref, keys_ext), (value_ref, values_ext))):
            send_if(
                seq < seqs - 1,
                src.at[tail],
                dst.at[pl.ds(0, window)],
                halo_send.at[n],
                halo_recv.at[n],
                {"seq": lax.rem(seq + 1, seqs)},
            )

    def send_states():
        for off in range(1, seqs):
            send_if(
                seq + off < seqs,
                state,
                state_in.at[off - 1],
                state_send.at[off - 1],
                state_recv.at[off - 1],
                {"seq": lax.rem(seq + off, seqs)},
            )

    def window_probs():
        @pl.when(seq > 0)
        def _():
            for n, dst in enumerate((keys_ext, values_ext)):
                arrived(dst.at[pl.ds(0, window)], halo_recv.at[n])

        shape = (rows, rows + window)
        query_pos = lax.broadcasted_iota(jnp.int32, shape, 0)
        key_pos = lax.broadcasted_iota(jnp.int32, shape, 1)
        allowed = (
            (key_pos > query_pos)
            & (key_pos <= query_pos + window)
            & (key_pos + (seq * rows - window) >= 0)
        )
        for h in range(heads):
            cols = of_head(h)
            scores = dot_t(query_ref[:, cols], keys_ext[:, cols]) * (HEAD_DIM**-0.5)
            scores = jnp.where(allowed, scores, -jnp.inf)
            weights = jnp.exp(scores - jnp.max(scores, axis=1, keepdims=True))
            softmax = weights / jnp.sum(weights, axis=1, keepdims=True)
            probs[h] = softmax
            attended[:, cols] = dot(softmax.astype(BF16), values_ext[:, cols])

    def states_before():
        for off in range(1, seqs):

            @pl.when(seq >= off)
            def _():
                arrived(state_in.at[off - 1], state_recv.at[off - 1])
                before[...] = before[...] + state_in[off - 1].astype(F32)

    fill(0)
    greet(("seq", "sub", "rep"))
    start(0)
    for c in range(1, chunks):
        fill(c)
    own_parts()
    columns = [as_column(place) for place in places]
    pair_weights = [as_column(weight_ref[k : k + 1, :]) for k in range(len(places))]
    left(0)
    if chunks > 1:
        start(1)
    for copy in weight_copies:
        copy.wait()
    for c in range(chunks + 2):
        if 2 <= c:
            forward(c - 2)
        if c < chunks:
            first_products(c)
        if c == chunks - 1:
            send_halos()
        if 1 <= c <= chunks:
            gate(c - 1)
        if c < chunks:
            chip_sums(c)
        if 2 <= c:
            second_products(c - 2)
    for batch in batches[1:]:
        sent.extend(batch)
    window_probs()

    combined = upstream_ref[...].astype(F32)
    for c in range(chunks):
        slot_at = lax.broadcasted_iota(jnp.int32, (rows, block), 1).astype(F32) + float(c * block)
        own[c].wait()
        for off in range(1, seqs):
            source = lax.rem(seq + seqs - off, seqs)
            arrived(returned.at[slot_rows(source, c)], out_recv.at[c, off - 1])
        for pair_weight, column in zip(pair_weights, columns):
            pick = (slot_at == column).astype(BF16)
            combined = combined + pair_weight * dot(
                pick, returned[c * block : (c + 1) * block, :]
            )
    resid = combined.astype(BF16)
    resid_ref[...] = resid

    def index_of(s, r):
        return s * reps + r

    def resid_on(sub_off):
        piece = index_of(lax.rem(sub + subs - sub_off, subs), rep)
        for off in range(1, reps):
            sent.append(
                send(
                    full.at[piece],
                    full.at[piece],
                    resr_send.at[off - 1, sub_off],
                    resr_recv.at[off - 1, sub_off],
                    {"rep": lax.rem(rep + off, reps)},
                )
            )

    def project(piece):
        cols = pl.ds(pl.multiple_of(piece * features, 128), features)
        return dot_t(full[piece], proj[:, cols])

    mine = index_of(sub, rep)
    full[mine] = resid
    for off in range(1, subs):
        sent.append(
            send(
                full.at[mine],
                full.at[mine],
                resx_send.at[off - 1],
                resx_recv.at[off - 1],
                {"sub": lax.rem(sub + off, subs)},
            )
        )
    resid_on(0)
    send_states()
    total = project(mine)
    for sub_off in range(subs):
        from_sub = lax.rem(sub + subs - sub_off, subs)
        if sub_off > 0:
            piece = index_of(from_sub, rep)
            arrived(full.at[piece], resx_recv.at[sub_off - 1])
            resid_on(sub_off)
            total = total + project(piece)
        for off in range(1, reps):
            piece = index_of(from_sub, lax.rem(rep + reps - off, reps))
            arrived(full.at[piece], resr_recv.at[off - 1, sub_off])
            total = total + project(piece)
    head_grad[...] = total.astype(BF16)

    for h in range(heads):
        cols = of_head(h)
        grad_state[h] = dot_0(query_ref[:, cols], head_grad[:, cols]).astype(BF16)
    parts = 2 if heads % 2 == 0 else 1
    passes = []
    for p in range(parts):
        some = pl.ds(p * (heads // parts), heads // parts)
        passes.append(
            pltpu.make_async_remote_copy(
                src_ref=grad_state.at[some],
                dst_ref=grad_state_in.at[some],
                send_sem=after_send.at[p],
                recv_sem=after_recv.at[p],
                device_id={"seq": lax.rem(seq + seqs - 1, seqs)},
                device_id_type=MESH,
            )
        )
        sent_if.append((seq > 0, passes[p]))

    def relay():
        for p in range(parts):
            some = pl.ds(p * (heads // parts), heads // parts)

            @pl.when(seq < seqs - 1)
            def _():
                arrived(grad_state_in.at[some], after_recv.at[p])
                later = grad_state_in[some].astype(F32)
                after[some] = later
                grad_state[some] = (grad_state[some].astype(F32) + later).astype(BF16)

            pl.when(seq > 0)(passes[p].start)

    scaling = HEAD_DIM**-0.5
    linear = float(HEAD_DIM * rows * seqs) ** -0.5
    causal = lax.broadcasted_iota(jnp.int32, (rows, rows), 0) >= lax.broadcasted_iota(
        jnp.int32, (rows, rows), 1
    )

    def window_part(h):
        cols = of_head(h)
        q, o = query_ref[:, cols], head_grad[:, cols]
        keys, values = keys_ext[:, cols], values_ext[:, cols]
        softmax = probs[h]
        centre = jnp.sum(o.astype(F32) * attended[:, cols], axis=1, keepdims=True)
        score_grad = (softmax * (dot_t(o, values) - centre)).astype(BF16)
        query_sum[:, cols] = dot(score_grad, keys) * scaling
        key_ext = dot_0(score_grad, q) * scaling
        value_ext = dot_0(softmax.astype(BF16), o)
        key_sum[:, cols] = key_ext[window:]
        value_sum[:, cols] = value_ext[window:]
        carry[0, :, cols] = key_ext[:window].astype(BF16)
        carry[1, :, cols] = value_ext[:window].astype(BF16)
        if h == heads - 1:
            send_if(
                seq > 0,
                carry,
                carry_in,
                carry_send.at[0],
                carry_recv.at[0],
                {"seq": lax.rem(seq + seqs - 1, seqs)},
            )

    def linear_part(h):
        cols = of_head(h)
        q, k, v, o = query_ref[:, cols], key_ref[:, cols], value_ref[:, cols], head_grad[:, cols]
        value_dots = jnp.where(causal, dot_t(o, v), 0.0).astype(BF16)
        query_sum[:, cols] = query_sum[:, cols] + linear * dot(value_dots, k)
        key_sum[:, cols] = key_sum[:, cols] + linear * dot_0(value_dots, q)
        value_sum[:, cols] = value_sum[:, cols] + linear * dot_0(query_dots[h], o)

    units = [functools.partial(window_part, h) for h in range(heads)]
    units += [functools.partial(linear_part, h) for h in range(heads)]
    turn = jnp.minimum(2 * (seqs - 1 - seq), len(units) - 1)
    for u, unit in enumerate(units):
        pl.when(turn == u)(relay)
        unit()

    states_before()
    for h in range(heads):
        cols = of_head(h)
        lin_query = dot_t(head_grad[:, cols], before[h].astype(BF16))
        query_grad_ref[:, cols] = (query_sum[:, cols] + linear * lin_query).astype(BF16)
    @pl.when(seq < seqs - 1)
    def _():
        arrived(carry_in, carry_recv.at[0])

    for h in range(heads):
        cols = of_head(h)
        k, v = key_ref[:, cols], value_ref[:, cols]
        later = after[h].astype(BF16)
        key_total = key_sum[:, cols] + linear * dot_t(v, later)
        value_total = value_sum[:, cols] + linear * dot(k, later)
        low = rows - window
        key_grad_ref[:low, cols] = key_total[:low].astype(BF16)
        value_grad_ref[:low, cols] = value_total[:low].astype(BF16)
        key_grad_ref[low:, cols] = (key_total[low:] + carry_in[0, :, cols].astype(F32)).astype(BF16)
        value_grad_ref[low:, cols] = (
            value_total[low:] + carry_in[1, :, cols].astype(F32)
        ).astype(BF16)
    for copy in sent:
        copy.wait_send()
    for cond, copy in sent_if:
        pl.when(cond)(copy.wait_send)


def local(
    moe_input,
    upstream,
    expert_ids,
    router_weight,
    w_gate,
    w_up,
    w_down,
    out_proj,
    query,
    key_in,
    value,
):
    rows, features = moe_input.shape
    seqs, subs, reps = lax.axis_size("seq"), lax.axis_size("sub"), lax.axis_size("rep")
    local_experts, _, hidden = w_gate.shape
    experts = local_experts * seqs
    cap = max(2, 3 * rows // experts)
    cap = -(-cap // 16) * 16
    while seqs * cap % (16 * subs * reps):
        cap += 16
    splits = SPLITS
    while cap % (16 * splits) or seqs * cap // splits % (16 * subs * reps):
        splits -= 1
    slot_count = experts * cap
    cap = cap // splits
    tile = 256 if hidden % 256 == 0 else hidden
    block = seqs * cap
    half_rows = block // reps
    piece_rows = half_rows // subs
    vmem = pl.BlockSpec(memory_space=pltpu.VMEM)
    hbm = pl.BlockSpec(memory_space=pl.ANY)
    dma = pltpu.SemaphoreType.DMA
    n = local_experts * splits
    heads = features // HEAD_DIM
    states = (heads, HEAD_DIM, HEAD_DIM)
    results = pl.pallas_call(
        functools.partial(kernel, cap, splits, tile),
        out_shape=[jax.ShapeDtypeStruct((rows, features), BF16)] * 4,
        in_specs=[vmem] * 7 + [hbm] * 4,
        out_specs=[vmem] * 4,
        scratch_shapes=[
            pltpu.VMEM((slot_count, 2 * features), BF16),
            pltpu.VMEM((n, block, 2 * features), BF16),
            pltpu.VMEM(w_gate.shape, BF16),
            pltpu.VMEM(w_up.shape, BF16),
            pltpu.VMEM(w_down.shape, BF16),
            pltpu.VMEM((n, 3, block, hidden), BF16),
            pltpu.VMEM((n, 3, reps - 1, half_rows, hidden), BF16),
            pltpu.VMEM((n, 3, half_rows, hidden), BF16),
            pltpu.VMEM((n, 3, subs - 1, piece_rows, hidden), BF16),
            pltpu.VMEM((n, block, 2 * hidden), BF16),
            pltpu.VMEM((n, block, features), BF16),
            pltpu.VMEM((slot_count, features), BF16),
            pltpu.VMEM(out_proj.shape, BF16),
            pltpu.VMEM((rows + WINDOW, features), BF16),
            pltpu.VMEM((rows + WINDOW, features), BF16),
            pltpu.VMEM((heads, rows, rows + WINDOW), F32),
            pltpu.VMEM((rows, features), F32),
            pltpu.VMEM((heads, rows, rows), BF16),
            pltpu.VMEM(states, BF16),
            pltpu.VMEM((seqs - 1,) + states, BF16),
            pltpu.VMEM(states, F32),
            pltpu.VMEM(states, BF16),
            pltpu.VMEM(states, BF16),
            pltpu.VMEM(states, F32),
            pltpu.VMEM((subs * reps, rows, features), BF16),
            pltpu.VMEM((rows, features), BF16),
            pltpu.VMEM((rows, features), F32),
            pltpu.VMEM((rows, features), F32),
            pltpu.VMEM((rows, features), F32),
            pltpu.VMEM((2, WINDOW, features), BF16),
            pltpu.VMEM((2, WINDOW, features), BF16),
            dma((4,)),
            dma((n,)),
            dma((n, seqs - 1)),
            dma((n, seqs - 1)),
            dma((n, 3, reps - 1)),
            dma((n, 3, reps - 1)),
            dma((n, 3, subs - 1)),
            dma((n, 3, subs - 1)),
            dma((n, subs - 1)),
            dma((n, subs - 1)),
            dma((n, reps - 1, subs)),
            dma((n, reps - 1, subs)),
            dma((n, seqs - 1)),
            dma((n, seqs - 1)),
            dma((2,)),
            dma((2,)),
            dma((seqs - 1,)),
            dma((seqs - 1,)),
            dma((2,)),
            dma((2,)),
            dma((subs - 1,)),
            dma((subs - 1,)),
            dma((reps - 1, subs)),
            dma((reps - 1, subs)),
            dma((1,)),
            dma((1,)),
        ],
        compiler_params=pltpu.CompilerParams(
            collective_id=0, has_side_effects=True, vmem_limit_bytes=56 * 1024 * 1024
        ),
        name="backward",
    )(
        expert_ids.T,
        router_weight.T,
        moe_input,
        upstream,
        query,
        key_in,
        value,
        w_gate,
        w_up,
        w_down,
        out_proj,
    )
    return pl.pallas_call(
        place_kernel,
        out_shape=[jax.ShapeDtypeStruct((rows, features), BF16)] * 4,
        in_specs=[vmem] * 4,
        out_specs=[vmem] * 4,
        name="place",
    )(*results)


def place_kernel(*refs):
    for src, dst in zip(refs[:4], refs[4:]):
        dst[...] = src[...]


def solution(mesh):
    return jax.shard_map(
        local,
        mesh=mesh,
        in_specs=(
            P(("groups", "seq"), ("sub", "rep")),
            P(("groups", "seq"), ("sub", "rep")),
            P(("groups", "seq"), None),
            P(("groups", "seq"), None),
            P("seq", ("sub", "rep"), None),
            P("seq", ("sub", "rep"), None),
            P("seq", None, ("sub", "rep")),
            P(("sub", "rep"), None),
            P(("groups", "seq"), ("sub", "rep")),
            P(("groups", "seq"), ("sub", "rep")),
            P(("groups", "seq"), ("sub", "rep")),
        ),
        out_specs=(
            P(("groups", "seq"), ("sub", "rep")),
            P(("groups", "seq"), ("sub", "rep")),
            P(("groups", "seq"), ("sub", "rep")),
            P(("groups", "seq"), ("sub", "rep")),
        ),
        check_vma=False,
    )
```
